256 devices in a mesh: rep: 64 (over z, x_hi, y), fsdp: 4 (over x_lo, core).
Axes of the slice: x: 4 (x_hi: 2, x_lo: 2; x = x_hi * 2 + x_lo), y: 4, z: 8, core: 2. Of those that a mesh axis runs over, the one named last changes fastest.
Arguments:
- inputs: bfloat16 [64, 2, 512, 2048], P('rep', None, 'fsdp'), may hold values from -6 to 6
- cotangent: bfloat16 [64, 2, 512, 2048], P('rep', None, 'fsdp'), may hold values from -6 to 6
- mid_gain: float32 [2048], replicated, may hold values from 0.5 to 1.5
- out_gain: float32 [2048], replicated, may hold values from 0.5 to 1.5
- up_weight: bfloat16 [64, 2048, 3584], P('rep', None, 'fsdp'), may hold values from -6 to 6
- down_weight: bfloat16 [64, 2048, 3584], P('rep', None, 'fsdp'), may hold values from -6 to 6
- up_rows: float32 [64, 2048], P('rep'), may hold values from 1e-09 to 1e-06
- up_cols: float32 [64, 3584], P('rep', 'fsdp'), may hold values from 1e-09 to 1e-06
- down_rows: float32 [64, 2048], P('rep'), may hold values from 1e-09 to 1e-06
- down_cols: float32 [64, 3584], P('rep', 'fsdp'), may hold values from 1e-09 to 1e-06
- anchor_up: float32 [2048, 512], P('rep', 'fsdp'), may hold values from -6 to 6
- anchor_down: float32 [2048, 512], P('rep', 'fsdp'), may hold values from -6 to 6
- momentum_up: float32 [2048, 512], P('rep', 'fsdp'), may hold values from -4 to 4
- momentum_down: float32 [2048, 512], P('rep', 'fsdp'), may hold values from -4 to 4
- fragment: int32 [1], replicated, may hold values from 0 to 6
Outputs:
- merged_up: bfloat16 [64, 2048, 512], P('rep', None, 'fsdp')
- merged_down: bfloat16 [64, 2048, 512], P('rep', None, 'fsdp')
- central_up: float32 [2048, 512], P('rep', 'fsdp')
- central_down: float32 [2048, 512], P('rep', 'fsdp')
- velocity_up: float32 [2048, 512], P('rep', 'fsdp')
- velocity_down: float32 [2048, 512], P('rep', 'fsdp')
- token_loss: float32 [64, 2, 512], P('rep', None, 'fsdp')
The draws below stay inside these ranges and needn't reach their ends.
All inputs are finite; a program needn't handle non-finite values.
Results may differ from the reference program's by a relative error of at most 0.002.
The reference program's roundings to bfloat16 on the way (of `normed`, `hidden`, `dbranch` and `dpre`) count: a program that leaves them out, or rounds other values in their place, can miss the bound.
Values may be sent and summed in bfloat16 or wider, within the bound.
A program may use at most 128 MiB of HBM per device.

```python
import math
import jax
import jax.numpy as jnp
from jax import lax

D = 2048
FRAGS = 7
HB_DEV = 128
FF = 3584
FRAG = 512
REPS = 64
TOKENS = 512
N_REP = 64
N_FSDP = 4


def levels(own_key, extent, pieces, smallest, high):
    loudness = 1.0
    for dim, parts in pieces:
        heights = jax.random.uniform(jax.random.fold_in(jax.random.fold_in(own_key, 6), dim), (parts,), jnp.float32, smallest / len(pieces), high / len(pieces))
        loudness = loudness * jnp.repeat(jnp.exp(heights), extent[dim] // parts).reshape((-1,) + (1,) * (len(extent) - 1 - dim))
    return loudness


def noise(own_key, dims, width, bound, split=(), held_as=jnp.bfloat16):
    factor_of = levels(own_key, dims, split, -0.22, 0.18) if split else 1.0
    result = jax.random.normal(own_key, dims, jnp.float32) * width * factor_of
    return jnp.minimum(jnp.maximum(result, -bound), bound).astype(held_as)


def setup_inputs(seed: int = 0) -> dict:
    splits = jax.random.split(jax.random.key(seed), 16)
    inputs = noise(splits[0], (REPS, 2, TOKENS, D), 1.0, 6.0, ((0, 64), (2, 4)))
    cotangent = noise(splits[1], (REPS, 2, TOKENS, D), 1.0, 6.0, ((0, 64), (2, 4)))
    mid_gain = jnp.clip(1.0 + 0.1 * jax.random.normal(splits[2], (D,), jnp.float32), 0.5, 1.5)
    out_gain = jnp.clip(1.0 + 0.1 * jax.random.normal(splits[3], (D,), jnp.float32), 0.5, 1.5)
    up_weight = noise(splits[4], (REPS, D, FF), 1.0, 6.0, ((0, 64), (2, 4)))
    down_weight = noise(splits[5], (REPS, D, FF), 1.0, 6.0, ((0, 64), (2, 4)))
    up_rows = jnp.clip(jnp.exp(math.log(9.999999974752427e-07) - 6.9077553 * jax.random.uniform(splits[6], (REPS, D), jnp.float32) ** levels(splits[6], (REPS, D), ((0, 64),), -0.2, 0.2)), 9.999999717180685e-10, 9.999999974752427e-07)
    up_cols = jnp.clip(jnp.exp(math.log(9.999999974752427e-07) - 6.9077553 * jax.random.uniform(splits[7], (REPS, FF), jnp.float32) ** levels(splits[7], (REPS, FF), ((0, 64), (1, 4)), -0.2, 0.2)), 9.999999717180685e-10, 9.999999974752427e-07)
    down_rows = jnp.clip(jnp.exp(math.log(9.999999974752427e-07) - 6.9077553 * jax.random.uniform(splits[8], (REPS, D), jnp.float32) ** levels(splits[8], (REPS, D), ((0, 64),), -0.2, 0.2)), 9.999999717180685e-10, 9.999999974752427e-07)
    down_cols = jnp.clip(jnp.exp(math.log(9.999999974752427e-07) - 6.9077553 * jax.random.uniform(splits[9], (REPS, FF), jnp.float32) ** levels(splits[9], (REPS, FF), ((0, 64), (1, 4)), -0.2, 0.2)), 9.999999717180685e-10, 9.999999974752427e-07)
    anchor_up = noise(splits[10], (D, FRAG), 1.0, 6.0, ((0, 64), (1, 4)), jnp.float32)
    anchor_down = noise(splits[11], (D, FRAG), 1.0, 6.0, ((0, 64), (1, 4)), jnp.float32)
    momentum_up = noise(splits[12], (D, FRAG), 0.3, 4.0, ((0, 64), (1, 4)), jnp.float32)
    momentum_down = noise(splits[13], (D, FRAG), 0.3, 4.0, ((0, 64), (1, 4)), jnp.float32)
    fragment = jax.random.randint(splits[14], (1,), 0, FRAGS).astype(jnp.int32)
    return {"inputs": inputs, "cotangent": cotangent, "mid_gain": mid_gain, "out_gain": out_gain, "up_weight": up_weight, "down_weight": down_weight, "up_rows": up_rows, "up_cols": up_cols, "down_rows": down_rows, "down_cols": down_cols, "anchor_up": anchor_up, "anchor_down": anchor_down, "momentum_up": momentum_up, "momentum_down": momentum_down, "fragment": fragment}


norm_epsilon = 1e-05
row_decay = 0.95
inner_rate = 0.05
weight_decay = 0.1
outer_rate = 0.7
outer_momentum = 0.9
mixing = 0.5

def normalize(values, gain):
    factor = lax.rsqrt(lax.optimization_barrier(jnp.mean(values * values, axis=-1, keepdims=True)) + norm_epsilon)
    return (values * factor * gain, factor)

def layer(inputs_now, cot_now, mid_gain, out_gain, up_now, down_now):
    residual = inputs_now.astype(jnp.float32)
    normed, mid_factor = normalize(residual, mid_gain)
    normed_low = normed.astype(jnp.bfloat16)
    preact = jnp.dot(normed_low, up_now, preferred_element_type=jnp.float32) * (1.0 / math.sqrt(D))
    logistic = jax.nn.sigmoid(preact)
    hidden = (preact * logistic).astype(jnp.bfloat16)
    branch = lax.dot_general(hidden, down_now, (((1,), (1,)), ((), ())), preferred_element_type=jnp.float32)
    output = residual + branch * (1.0 / math.sqrt(FF))
    final, out_factor = normalize(output, out_gain)
    losses = lax.optimization_barrier(jnp.sum(cot_now.astype(jnp.float32) * final, axis=-1))
    return (losses, normed_low, preact, logistic, hidden, output, out_factor)

def factored_update(weight, rows, cols, gradient):
    squared = gradient * gradient
    rows_new = row_decay * rows + (1 - row_decay) * lax.optimization_barrier(jnp.mean(squared, axis=1))
    cols_new = row_decay * cols + (1 - row_decay) * lax.optimization_barrier(jnp.mean(squared, axis=0))
    estimate = rows_new[:, None] * cols_new[None, :] / jnp.mean(rows_new)
    weight_full = weight.astype(jnp.float32)
    weight_full = weight_full - inner_rate * (gradient * lax.rsqrt(estimate) + weight_decay * weight_full)
    return weight_full.astype(jnp.bfloat16)

def fragment_block(weights, index):
    shaped = weights.reshape(weights.shape[:-1] + (N_FSDP, FRAGS, HB_DEV))
    picked = lax.dynamic_index_in_dim(shaped, index, axis=weights.ndim, keepdims=False)
    return picked.reshape(weights.shape[:-1] + (FRAG,))

def reference(inputs, cotangent, mid_gain, out_gain, up_weight, down_weight, up_rows, up_cols, down_rows, down_cols, anchor_up, anchor_down, momentum_up, momentum_down, fragment):
    index = fragment[0].astype(jnp.int32)
    total_up = lax.optimization_barrier(jnp.sum(fragment_block(up_weight, index).astype(jnp.float32), axis=0))
    total_down = lax.optimization_barrier(jnp.sum(fragment_block(down_weight, index).astype(jnp.float32), axis=0))
    drift_up = anchor_up - total_up / N_REP
    drift_down = anchor_down - total_down / N_REP
    velocity_up = outer_momentum * momentum_up + drift_up
    velocity_down = outer_momentum * momentum_down + drift_down
    central_up = anchor_up - outer_rate * (drift_up + outer_momentum * velocity_up)
    central_down = anchor_down - outer_rate * (drift_down + outer_momentum * velocity_down)

    def one_replica(packed):
        batch, cots, up_now, down_now, rows_up, cols_up, rows_down, cols_down = packed
        first, normed_low, preact, logistic, hidden, output, out_factor = layer(batch[0], cots[0], mid_gain, out_gain, up_now, down_now)
        gscaled = cots[0].astype(jnp.float32) * (1.0 / TOKENS) * out_gain
        doutput = out_factor * gscaled - output * out_factor ** 3 * lax.optimization_barrier(jnp.mean(output * gscaled, axis=-1, keepdims=True))
        dbranch = (doutput * (1.0 / math.sqrt(FF))).astype(jnp.bfloat16)
        grad_down = lax.dot_general(dbranch, hidden, (((0,), (0,)), ((), ())), preferred_element_type=jnp.float32)
        dhidden = jnp.dot(dbranch, down_now, preferred_element_type=jnp.float32)
        dpre = (dhidden * logistic * (1 + preact * (1 - logistic)) * (1.0 / math.sqrt(D))).astype(jnp.bfloat16)
        grad_up = lax.dot_general(normed_low, dpre, (((0,), (0,)), ((), ())), preferred_element_type=jnp.float32)
        up_new = factored_update(up_now, rows_up, cols_up, grad_up)
        down_new = factored_update(down_now, rows_down, cols_down, grad_down)
        second = layer(batch[1], cots[1], mid_gain, out_gain, up_new, down_new)[0]
        return (jnp.stack([first, second]), fragment_block(up_new, index), fragment_block(down_new, index))
    token_loss, block_up, block_down = lax.map(one_replica, (inputs, cotangent, up_weight, down_weight, up_rows, up_cols, down_rows, down_cols))
    merged_up = (mixing * block_up.astype(jnp.float32) + (1 - mixing) * central_up[None]).astype(jnp.bfloat16)
    merged_down = (mixing * block_down.astype(jnp.float32) + (1 - mixing) * central_down[None]).astype(jnp.bfloat16)
    return (merged_up, merged_down, central_up, central_down, velocity_up, velocity_down, token_loss)
```

```python
import functools
import math

import jax
import jax.numpy as jnp
from jax import lax
from jax.experimental import pallas as pl
from jax.experimental.pallas import tpu as pltpu
from jax.sharding import PartitionSpec as P

norm_epsilon = 1e-05
row_decay = 0.95
inner_rate = 0.05
weight_decay = 0.1
outer_rate = 0.7
outer_momentum = 0.9
mixing = 0.5

F32 = jnp.float32
BF16 = jnp.bfloat16
CHUNKS = 4


def mm(a, b):
    return jnp.dot(a, b, preferred_element_type=F32)


def mm_nt(a, b):
    return lax.dot_general(a, b, (((1,), (1,)), ((), ())), preferred_element_type=F32)


def mm_tn(a, b):
    return lax.dot_general(a, b, (((0,), (0,)), ((), ())), preferred_element_type=F32)


def pieces(extent, size):
    return [(s, min(size, extent - s)) for s in range(0, extent, size)]


def kernel(
    reps_z,
    reps_xy,
    frag,
    x_in,
    cot,
    mid_gain,
    out_gain,
    up_hbm,
    down_hbm,
    up_rows,
    up_cols,
    down_rows,
    down_cols,
    anchor_up,
    anchor_down,
    moment_up,
    moment_down,
    merged_up,
    merged_down,
    central_up,
    central_down,
    velocity_up,
    velocity_down,
    loss,
    up,
    down,
    x0,
    x1,
    db,
    slope,
    hid,
    dpre,
    part,
    from_sib0,
    from_sib1,
    to_peer0,
    to_peer1,
    from_peer0,
    from_peer1,
    grad_up,
    grad_down,
    block,
    from_z,
    sum_z,
    from_xy,
    central,
    rows_out,
    rows_in,
    cols_acc,
    load_sem,
    gather_sem,
    part_sem,
    rows_sem,
    z_sem,
    xy_sem,
    cxy_sem,
    cz_sem,
):
    width, units_here = up.shape
    tok = x_in.shape[1]
    shards = 4
    units = units_here * shards
    tokens = tok * shards
    reps = reps_z * reps_xy
    half = 2 * tok
    bw = block.shape[2]

    rep = lax.axis_index("rep")
    f = lax.axis_index("fsdp")
    z = rep // reps_xy
    xy = rep % reps_xy
    chip = f // 2
    core = f % 2
    sib = {"rep": rep, "fsdp": chip * 2 + (1 - core)}
    peer = {"rep": rep, "fsdp": (1 - chip) * 2 + core}
    diag = {"rep": rep, "fsdp": (1 - chip) * 2 + (1 - core)}

    def at_z(step):
        other = (z + step) % reps_z
        return other, {"rep": other * reps_xy + xy, "fsdp": f}

    def at_xy(step):
        other = (xy + step) % reps_xy
        return other, {"rep": z * reps_xy + other, "fsdp": f}

    sent = []

    def send(src, dst, sems, target):
        copy = pltpu.make_async_remote_copy(
            src_ref=src,
            dst_ref=dst,
            send_sem=sems.at[0],
            recv_sem=sems.at[1],
            device_id=target,
            device_id_type=pl.DeviceIdType.MESH,
        )
        copy.start()
        sent.append(copy)
        return copy

    load_up = pltpu.make_async_copy(up_hbm, up, load_sem.at[0])
    load_down = pltpu.make_async_copy(down_hbm, down, load_sem.at[1])
    load_up.start()
    load_down.start()

    barrier = pltpu.get_barrier_semaphore()
    partners = [sib, peer, diag]
    partners += [at_z(s)[1] for s in range(1, reps_z)]
    partners += [at_xy(s)[1] for s in range(1, reps_xy)]
    for partner in partners:
        pl.semaphore_signal(
            barrier, inc=1, device_id=partner, device_id_type=pl.DeviceIdType.MESH
        )

    rows_each = tok // CHUNKS

    def normalize_chunk(batch, dst, c):
        rows = slice(c * rows_each, (c + 1) * rows_each)
        v = x_in[batch, rows, :].astype(F32)
        factor = lax.rsqrt(jnp.mean(v * v, axis=-1, keepdims=True) + norm_epsilon)
        dst[rows, :] = (v * factor * mid_gain[...]).astype(BF16)

    def spread(buf, g, c):
        r = pl.ds(c * rows_each, rows_each)
        over = send(
            buf.at[r, :],
            buf.at[pl.ds(half + c * rows_each, rows_each), :],
            gather_sem.at[g, 1, c],
            peer,
        )
        near = send(
            buf.at[r, :],
            buf.at[pl.ds(tok + c * rows_each, rows_each), :],
            gather_sem.at[g, 0, c],
            sib,
        )
        return near, over

    def forward(buf, g, c, over):
        over.wait_recv()
        return send(
            buf.at[pl.ds(half + c * rows_each, rows_each), :],
            buf.at[pl.ds(half + tok + c * rows_each, rows_each), :],
            gather_sem.at[g, 2, c],
            sib,
        )

    for c in range(CHUNKS):
        normalize_chunk(0, x0, c)
    pl.semaphore_wait(barrier, len(partners))
    pairs0 = [spread(x0, 0, c) for c in range(CHUNKS)]

    strip = min(width, 256)
    chosen = [
        jnp.full((strip, bw), jnp.where(frag[0] == k, 1.0, 0.0), F32).astype(BF16)
        for k in range(units_here // bw)
    ]

    def fragment_rows(weight, k):
        rows = pl.ds(k, strip)
        picked = weight[rows, 0:bw] * chosen[0]
        for n in range(1, units_here // bw):
            picked = picked + weight[rows, n * bw : (n + 1) * bw] * chosen[n]
        return picked

    load_up.wait()
    load_down.wait()
    for k in range(0, width, strip):
        block[0, k : k + strip, :] = fragment_rows(up, k)
        block[1, k : k + strip, :] = fragment_rows(down, k)
    span_z = width // reps_z
    span = width // reps
    z_copies = []
    for s in range(1, reps_z):
        other, target = at_z(s)
        z_copies.append(
            send(
                block.at[:, pl.ds(other * span_z, span_z), :],
                from_z.at[s - 1],
                z_sem.at[s - 1],
                target,
            )
        )

    def sum_over_z():
        for w in range(2):
            total = block[w, pl.ds(z * span_z, span_z), :].astype(F32)
            for s in range(1, reps_z):
                if w == 0:
                    z_copies[s - 1].wait_recv()
                total = total + from_z[s - 1, w].astype(F32)
            sum_z[w] = total
        copies = []
        for s in range(1, reps_xy):
            other, target = at_xy(s)
            copies.append(
                send(
                    sum_z.at[:, pl.ds(other * span, span), :],
                    from_xy.at[s - 1],
                    xy_sem.at[s - 1],
                    target,
                )
            )
        return copies

    def outer_step(copies):
        for copy in copies:
            copy.wait_recv()
        mine = pl.ds(rep * span, span)
        for w, (anchor, moment, cent_out, vel_out) in enumerate(
            (
                (anchor_up, moment_up, central_up, velocity_up),
                (anchor_down, moment_down, central_down, velocity_down),
            )
        ):
            total = sum_z[w, pl.ds(xy * span, span), :]
            for s in range(1, reps_xy):
                total = total + from_xy[s - 1, w]
            drift = anchor[...] - total / reps
            velocity = outer_momentum * moment[...] + drift
            cent = anchor[...] - outer_rate * (drift + outer_momentum * velocity)
            vel_out[...] = velocity
            cent_out[...] = cent
            central[w, mine, :] = cent
        out = []
        for s in range(1, reps_xy):
            _, target = at_xy(s)
            out.append(
                send(central.at[:, mine, :], central.at[:, mine, :], cxy_sem.at[s - 1], target)
            )
        return out

    def gather_over_z(copies):
        for copy in copies:
            copy.wait_recv()
        slab = pl.ds(z * span_z, span_z)
        out = []
        for s in range(1, reps_z):
            _, target = at_z(s)
            out.append(
                send(central.at[:, slab, :], central.at[:, slab, :], cz_sem.at[s - 1], target)
            )
        return out

    def hidden_of(buf, lo, count, keep_slope):
        rows = slice(lo, lo + count)
        for n, size in pieces(units_here, 256):
            pre = mm(buf[rows, :], up[:, n : n + size]) * (1.0 / math.sqrt(width))
            sig = jax.nn.sigmoid(pre)
            hid[rows, n : n + size] = (pre * sig).astype(BF16)
            if keep_slope:
                slope[rows, n : n + size] = (
                    sig * (1 + pre * (1 - sig)) * (1.0 / math.sqrt(width))
                )

    feats = width // CHUNKS

    def branch_of(lo, count, j):
        part[lo : lo + count, j * feats : (j + 1) * feats] = mm_nt(
            hid[lo : lo + count, :], down[j * feats : (j + 1) * feats, :]
        )

    def sib_send(b, which, j, dst):
        lo = tok + which * half
        cols = pl.ds(j * feats, feats)
        return send(
            part.at[pl.ds(lo, tok), cols],
            dst.at[which, :, cols],
            part_sem.at[b, which, j],
            sib,
        )

    def peer_send(b, j, copy, src_sib, staged, dst):
        copy.wait_recv()
        cols = slice(j * feats, (j + 1) * feats)
        staged[:, cols] = (part[half : half + tok, cols] + src_sib[1, :, cols]).astype(BF16)
        ds = pl.ds(j * feats, feats)
        return send(staged.at[:, ds], dst.at[:, ds], part_sem.at[b, 2, j], peer)

    def lanes_of(column_vector):
        wide = jnp.broadcast_to(column_vector, (tok, 128))
        return jnp.transpose(wide)[0:1, :]

    for near, _ in pairs0:
        near.wait_recv()
    hidden_of(x0, 0, half, True)
    diag0 = []
    near_part0 = []
    for j in range(CHUNKS):
        branch_of(0, half, j)
        near_part0.append(sib_send(0, 0, j, from_sib0))
        diag0.append(forward(x0, 0, j, pairs0[j][1]))
    for copy in diag0:
        copy.wait_recv()
    hidden_of(x0, half, half, True)
    far_part0 = []
    over_part0 = []
    for j in range(CHUNKS):
        branch_of(half, half, j)
        far_part0.append(sib_send(0, 1, j, from_sib0))
        if j:
            over_part0.append(
                peer_send(0, j - 1, far_part0[j - 1], from_sib0, to_peer0, from_peer0)
            )
    over_part0.append(
        peer_send(0, CHUNKS - 1, far_part0[-1], from_sib0, to_peer0, from_peer0)
    )
    for c in range(CHUNKS):
        normalize_chunk(1, x1, c)
    xy_copies = sum_over_z()
    for copy in near_part0 + over_part0:
        copy.wait_recv()

    def output_of(b, c, src_sib, src_peer):
        rows = slice(c * rows_each, (c + 1) * rows_each)
        branch = part[rows, :] + src_sib[0, rows, :] + src_peer[rows, :].astype(F32)
        output = x_in[b, rows, :].astype(F32) + branch * (1.0 / math.sqrt(units))
        q = lax.rsqrt(jnp.mean(output * output, axis=-1, keepdims=True) + norm_epsilon)
        c_gain = cot[b, rows, :].astype(F32) * out_gain[...]
        dotted = jnp.sum(c_gain * output, axis=-1, keepdims=True)
        return output, q, c_gain, dotted

    def token_losses(columns):
        return lanes_of(jnp.concatenate(columns, axis=0))

    pairs_d = []
    losses = []
    for c in range(CHUNKS):
        output, q, c_gain, dotted = output_of(0, c, from_sib0, from_peer0)
        losses.append(dotted * q)
        g = c_gain * (1.0 / tokens)
        doutput = q * g - output * (q * q * q * (dotted * (1.0 / (tokens * width))))
        db[c * rows_each : (c + 1) * rows_each, :] = (
            doutput * (1.0 / math.sqrt(units))
        ).astype(BF16)
        pairs_d.append(spread(db, 1, c))
    loss[0:1, :] = token_losses(losses)
    cxy_copies = outer_step(xy_copies)

    def dpre_of(lo, count):
        rows = slice(lo, lo + count)
        for n, size in pieces(units_here, 256):
            dh = mm(db[rows, :], down[:, n : n + size])
            dpre[rows, n : n + size] = (dh * slope[rows, n : n + size]).astype(BF16)

    step = 256
    n_steps = width // step

    def first_half(dst, left, right):
        def body(i, carry):
            k = pl.multiple_of(i * step, step)
            dst[pl.ds(k, step), :] = mm_tn(left[0:half, pl.ds(k, step)], right[0:half, :])
            return carry

        lax.fori_loop(0, n_steps, body, 0)

    def second_half(w, dst, left, right):
        cols_acc[w] = jnp.zeros((1, units_here), F32)

        def body(i, carry):
            k = pl.multiple_of(i * step, step)
            g = dst[pl.ds(k, step), :] + mm_tn(
                left[half : 2 * half, pl.ds(k, step)], right[half : 2 * half, :]
            )
            dst[pl.ds(k, step), :] = g
            sq = g * g
            cols_acc[w] += jnp.sum(sq, axis=0, keepdims=True)
            lanes = sq[:, 0:128]
            for s in range(128, units_here, 128):
                lanes = lanes + sq[:, s : s + 128]
            rows_out[w, :, pl.ds(k, step)] = jnp.sum(
                jnp.transpose(lanes), axis=0, keepdims=True
            )
            return carry

        lax.fori_loop(0, n_steps, body, 0)
        return [
            send(rows_out.at[w], rows_in.at[w, i], rows_sem.at[w, i], target)
            for i, target in enumerate((sib, peer, diag))
        ]

    for near, _ in pairs_d:
        near.wait_recv()
    dpre_of(0, half)
    diag_d = [forward(db, 1, 0, pairs_d[0][1])]
    first_half(grad_up, x0, dpre)
    diag_d.append(forward(db, 1, 1, pairs_d[1][1]))
    first_half(grad_down, db, hid)
    for c in range(2, CHUNKS):
        diag_d.append(forward(db, 1, c, pairs_d[c][1]))
    cz_copies = gather_over_z(cxy_copies)
    for copy in diag_d:
        copy.wait_recv()
    pairs1 = [spread(x1, 2, c) for c in range(CHUNKS)]
    dpre_of(half, half)
    rows_up_copies = second_half(0, grad_up, x0, dpre)
    diag1 = [forward(x1, 2, c, pairs1[c][1]) for c in range(2)]
    rows_down_copies = second_half(1, grad_down, db, hid)

    def factors(w, copies, rows_ref, cols_ref):
        for copy in copies:
            copy.wait_recv()
        total = rows_out[w] + rows_in[w, 0] + rows_in[w, 1] + rows_in[w, 2]
        rows2 = row_decay * rows_ref[...] + ((1 - row_decay) / units) * total
        cols2 = row_decay * cols_ref[...] + ((1 - row_decay) / width) * cols_acc[w]
        mean = jnp.mean(rows2, axis=-1, keepdims=True)
        rows_in[w, 0] = lax.rsqrt(rows2) * inner_rate
        cols_acc[w] = lax.rsqrt(cols2 / mean)

    def update(w, weight, grad, k, size):
        scale = jnp.transpose(
            jnp.broadcast_to(rows_in[w, 0, :, pl.ds(k, size)], (128, size))
        )
        for s in range(0, units_here, 128):
            move = grad[pl.ds(k, size), s : s + 128] * scale * cols_acc[w, :, s : s + 128]
            old = weight[pl.ds(k, size), s : s + 128].astype(F32)
            weight[pl.ds(k, size), s : s + 128] = (
                old * (1 - inner_rate * weight_decay) - move
            ).astype(BF16)

    def update_all(w, weight, grad):
        def body(i, carry):
            update(w, weight, grad, pl.multiple_of(i * step, step), step)
            return carry

        lax.fori_loop(0, n_steps, body, 0)

    factors(0, rows_up_copies, up_rows, up_cols)
    update_all(0, up, grad_up)
    diag1 += [forward(x1, 2, c, pairs1[c][1]) for c in range(2, CHUNKS)]
    for (near, _), far in zip(pairs1, diag1):
        near.wait_recv()
        far.wait_recv()
    hidden_of(x1, 0, 2 * half, False)
    factors(1, rows_down_copies, down_rows, down_cols)
    for copy in near_part0 + far_part0:
        copy.wait_send()
        sent[:] = [other for other in sent if other is not copy]
    near_part1 = []
    far_part1 = []
    over_part1 = []
    for j in range(CHUNKS):
        for k, size in pieces(feats, step):
            update(1, down, grad_down, j * feats + k, size)
        branch_of(0, 2 * half, j)
        far_part1.append(sib_send(1, 1, j, from_sib1))
        near_part1.append(sib_send(1, 0, j, from_sib1))
        if j:
            over_part1.append(
                peer_send(1, j - 1, far_part1[j - 1], from_sib1, to_peer1, from_peer1)
            )
    over_part1.append(
        peer_send(1, CHUNKS - 1, far_part1[-1], from_sib1, to_peer1, from_peer1)
    )

    for copy in cz_copies:
        copy.wait_recv()
    for k in range(0, width, strip):
        for w, (weight, merged) in enumerate(((up, merged_up), (down, merged_down))):
            merged[k : k + strip, :] = (
                mixing * fragment_rows(weight, k).astype(F32)
                + (1 - mixing) * central[w, k : k + strip, :]
            ).astype(BF16)

    for copy in near_part1 + over_part1:
        copy.wait_recv()
    losses = []
    for c in range(CHUNKS):
        _, q, _, dotted = output_of(1, c, from_sib1, from_peer1)
        losses.append(dotted * q)
    loss[1:2, :] = token_losses(losses)
    for copy in sent:
        copy.wait_send()


def per_device(reps_z, reps_xy, inputs, cotangent, mid_gain, out_gain, up_weight, down_weight,
               up_rows, up_cols, down_rows, down_cols, anchor_up, anchor_down,
               momentum_up, momentum_down, fragment):
    _, _, tok, width = inputs.shape
    units_here = up_weight.shape[2]
    span, bw = anchor_up.shape
    reps = reps_z * reps_xy
    tokens = 4 * tok
    vmem = pl.BlockSpec(memory_space=pltpu.VMEM)
    hbm = pl.BlockSpec(memory_space=pl.ANY)
    smem = pl.BlockSpec(memory_space=pltpu.SMEM)
    flops = 7 * 2 * tokens * width * units_here
    results = pl.pallas_call(
        functools.partial(kernel, reps_z, reps_xy),
        out_shape=(
            jax.ShapeDtypeStruct((width, bw), BF16),
            jax.ShapeDtypeStruct((width, bw), BF16),
            jax.ShapeDtypeStruct((span, bw), F32),
            jax.ShapeDtypeStruct((span, bw), F32),
            jax.ShapeDtypeStruct((span, bw), F32),
            jax.ShapeDtypeStruct((span, bw), F32),
            jax.ShapeDtypeStruct((2, tok), F32),
        ),
        in_specs=[smem, vmem, vmem, vmem, vmem, hbm, hbm] + [vmem] * 8,
        out_specs=tuple([vmem] * 7),
        scratch_shapes=[
            pltpu.VMEM((width, units_here), BF16),
            pltpu.VMEM((width, units_here), BF16),
            pltpu.VMEM((tokens, width), BF16),
            pltpu.VMEM((tokens, width), BF16),
            pltpu.VMEM((tokens, width), BF16),
            pltpu.VMEM((tokens, units_here), F32),
            pltpu.VMEM((tokens, units_here), BF16),
            pltpu.VMEM((tokens, units_here), BF16),
            pltpu.VMEM((tokens, width), F32),
            pltpu.VMEM((2, tok, width), F32),
            pltpu.VMEM((2, tok, width), F32),
            pltpu.VMEM((tok, width), BF16),
            pltpu.VMEM((tok, width), BF16),
            pltpu.VMEM((tok, width), BF16),
            pltpu.VMEM((tok, width), BF16),
            pltpu.VMEM((width, units_here), F32),
            pltpu.VMEM((width, units_here), F32),
            pltpu.VMEM((2, width, bw), BF16),
            pltpu.VMEM((reps_z - 1, 2, width // reps_z, bw), BF16),
            pltpu.VMEM((2, width // reps_z, bw), F32),
            pltpu.VMEM((reps_xy - 1, 2, span, bw), F32),
            pltpu.VMEM((2, width, bw), F32),
            pltpu.VMEM((2, 1, width), F32),
            pltpu.VMEM((2, 3, 1, width), F32),
            pltpu.VMEM((2, 1, units_here), F32),
            pltpu.SemaphoreType.DMA((2,)),
            pltpu.SemaphoreType.DMA((3, 3, CHUNKS, 2)),
            pltpu.SemaphoreType.DMA((2, 3, CHUNKS, 2)),
            pltpu.SemaphoreType.DMA((2, 3, 2)),
            pltpu.SemaphoreType.DMA((reps_z - 1, 2)),
            pltpu.SemaphoreType.DMA((reps_xy - 1, 2)),
            pltpu.SemaphoreType.DMA((reps_xy - 1, 2)),
            pltpu.SemaphoreType.DMA((reps_z - 1, 2)),
        ],
        compiler_params=pltpu.CompilerParams(
            collective_id=0,
            has_side_effects=True,
            vmem_limit_bytes=62 * 1024 * 1024,
        ),
        cost_estimate=pl.CostEstimate(
            flops=flops, bytes_accessed=10_000_000, transcendentals=0
        ),
        name="window",
    )(
        fragment,
        inputs[0],
        cotangent[0],
        mid_gain[None],
        out_gain[None],
        up_weight[0],
        down_weight[0],
        up_rows,
        up_cols,
        down_rows,
        down_cols,
        anchor_up,
        anchor_down,
        momentum_up,
        momentum_down,
    )
    merged_up, merged_down, c_up, c_down, v_up, v_down, loss = results
    return merged_up[None], merged_down[None], c_up, c_down, v_up, v_down, loss[None]


def solution(mesh):
    reps = mesh.shape["rep"]
    reps_xy = 8 if reps % 8 == 0 and reps > 8 else 2
    reps_z = reps // reps_xy
    placed = (
        P("rep", None, "fsdp", None),
        P("rep", None, "fsdp", None),
        P(),
        P(),
        P("rep", None, "fsdp"),
        P("rep", None, "fsdp"),
        P("rep", None),
        P("rep", "fsdp"),
        P("rep", None),
        P("rep", "fsdp"),
        P("rep", "fsdp"),
        P("rep", "fsdp"),
        P("rep", "fsdp"),
        P("rep", "fsdp"),
        P(),
    )
    return jax.shard_map(
        functools.partial(per_device, reps_z, reps_xy),
        mesh=mesh,
        in_specs=placed,
        out_specs=(
            P("rep", None, "fsdp"),
            P("rep", None, "fsdp"),
            P("rep", "fsdp"),
            P("rep", "fsdp"),
            P("rep", "fsdp"),
            P("rep", "fsdp"),
            P("rep", None, "fsdp"),
        ),
        check_vma=False,
    )
```

```python
import functools
import math

import jax
import jax.numpy as jnp
from jax import lax
from jax.experimental import pallas as pl
from jax.experimental.pallas import tpu as pltpu
from jax.sharding import PartitionSpec as P

norm_epsilon = 1e-05
row_decay = 0.95
inner_rate = 0.05
weight_decay = 0.1
outer_rate = 0.7
outer_momentum = 0.9
mixing = 0.5

F32 = jnp.float32
BF16 = jnp.bfloat16
CHUNKS = 4


def mm(a, b):
    return jnp.dot(a, b, preferred_element_type=F32)


def mm_nt(a, b):
    return lax.dot_general(a, b, (((1,), (1,)), ((), ())), preferred_element_type=F32)


def mm_tn(a, b):
    return lax.dot_general(a, b, (((0,), (0,)), ((), ())), preferred_element_type=F32)


def pieces(extent, size):
    return [(s, min(size, extent - s)) for s in range(0, extent, size)]


def kernel(
    reps_z,
    reps_y,
    frag,
    x_in,
    cot,
    mid_gain,
    out_gain,
    up_hbm,
    down_hbm,
    up_rows,
    up_cols,
    down_rows,
    down_cols,
    anchor_up,
    anchor_down,
    moment_up,
    moment_down,
    merged_up,
    merged_down,
    central_up,
    central_down,
    velocity_up,
    velocity_down,
    loss,
    up,
    down,
    x0,
    x1,
    db,
    slope,
    hid,
    dpre,
    part,
    from_sib0,
    from_sib1,
    to_peer0,
    to_peer1,
    from_peer0,
    from_peer1,
    grad_up,
    grad_down,
    block,
    up_from_y,
    up_y,
    up_from_z,
    down_from_z,
    down_z,
    down_from_y,
    pair,
    from_x,
    central,
    rows_out,
    rows_in,
    cols_acc,
    load_sem,
    gather_sem,
    part_sem,
    rows_sem,
    a_sem,
    b_sem,
    c_sem,
    e_sem,
    f_sem,
):
    width, units_here = up.shape
    tok = x_in.shape[1]
    shards = 4
    units = units_here * shards
    tokens = tok * shards
    reps = reps_z * 2 * reps_y
    half = 2 * tok
    bw = block.shape[4]

    rep = lax.axis_index("rep")
    f = lax.axis_index("fsdp")
    z = rep // (2 * reps_y)
    xh = rep // reps_y % 2
    y = rep % reps_y
    chip = f // 2
    core = f % 2
    sib = {"rep": rep, "fsdp": chip * 2 + (1 - core)}
    peer = {"rep": rep, "fsdp": (1 - chip) * 2 + core}
    diag = {"rep": rep, "fsdp": (1 - chip) * 2 + (1 - core)}

    def device(z_, xh_, y_):
        return {"rep": (z_ * 2 + xh_) * reps_y + y_, "fsdp": f}

    across = device(z, 1 - xh, y)
    others_z = [(z + s) % reps_z for s in range(1, reps_z)]
    others_y = [(y + s) % reps_y for s in range(1, reps_y)]

    sent = []

    def send(src, dst, sems, target):
        copy = pltpu.make_async_remote_copy(
            src_ref=src,
            dst_ref=dst,
            send_sem=sems.at[0],
            recv_sem=sems.at[1],
            device_id=target,
            device_id_type=pl.DeviceIdType.MESH,
        )
        copy.start()
        sent.append(copy)
        return copy

    load_up = pltpu.make_async_copy(up_hbm, up, load_sem.at[0])
    load_down = pltpu.make_async_copy(down_hbm, down, load_sem.at[1])
    load_up.start()
    load_down.start()

    barrier = pltpu.get_barrier_semaphore()
    partners = [sib, peer, diag]
    partners += [device(o, xh, y) for o in others_z]
    partners += [device(z, xh, o) for o in others_y]
    partners += [across]
    for partner in partners:
        pl.semaphore_signal(
            barrier, inc=1, device_id=partner, device_id_type=pl.DeviceIdType.MESH
        )

    rows_each = tok // CHUNKS

    def normalize_chunk(batch, dst, c):
        rows = slice(c * rows_each, (c + 1) * rows_each)
        v = x_in[batch, rows, :].astype(F32)
        factor = lax.rsqrt(jnp.mean(v * v, axis=-1, keepdims=True) + norm_epsilon)
        dst[rows, :] = (v * factor * mid_gain[...]).astype(BF16)

    def spread(buf, g, c):
        r = pl.ds(c * rows_each, rows_each)
        over = send(
            buf.at[r, :],
            buf.at[pl.ds(half + c * rows_each, rows_each), :],
            gather_sem.at[g, 1, c],
            peer,
        )
        near = send(
            buf.at[r, :],
            buf.at[pl.ds(tok + c * rows_each, rows_each), :],
            gather_sem.at[g, 0, c],
            sib,
        )
        return near, over

    def forward(buf, g, c, over):
        over.wait_recv()
        return send(
            buf.at[pl.ds(half + c * rows_each, rows_each), :],
            buf.at[pl.ds(half + tok + c * rows_each, rows_each), :],
            gather_sem.at[g, 2, c],
            sib,
        )

    for c in range(CHUNKS):
        normalize_chunk(0, x0, c)
    pl.semaphore_wait(barrier, len(partners))
    pairs0 = [spread(x0, 0, c) for c in range(CHUNKS)]

    chosen = [jnp.where(frag[0] == k, 1.0, 0.0) for k in range(units_here // bw)]

    def fragment_rows(weight, k, strip):
        rows = pl.ds(k, strip)
        picked = None
        for n, one in enumerate(chosen):
            term = weight[rows, n * bw : (n + 1) * bw] * jnp.full(
                (strip, bw), one, F32
            ).astype(BF16)
            picked = term if picked is None else picked + term
        return picked

    load_up.wait()
    load_down.wait()
    span = width // reps
    slab = reps_y * span
    for k in range(0, width, slab):
        block[0, k // slab] = fragment_rows(up, k, slab).reshape(reps_y, span, bw)
        block[1, k // slab] = fragment_rows(down, k, slab).reshape(reps_y, span, bw)
    here = pl.ds(z * 2, 2)

    def spread_blocks():
        over_y = [
            send(block.at[0, :, o], up_from_y.at[i], a_sem.at[0, i], device(z, xh, o))
            for i, o in enumerate(others_y)
        ]
        over_z = [
            send(
                block.at[1, pl.ds(o * 2, 2)],
                down_from_z.at[i],
                a_sem.at[1, i],
                device(o, xh, y),
            )
            for i, o in enumerate(others_z)
        ]
        return over_y, over_z

    def sum_once(copies):
        over_y, over_z = copies
        for copy in over_y:
            copy.wait_recv()
        total = block[0, :, y].astype(F32)
        for i in range(reps_y - 1):
            total = total + up_from_y[i].astype(F32)
        up_y[...] = total
        up_z_copies = [
            send(
                up_y.at[pl.ds(o * 2, 2)], up_from_z.at[i], b_sem.at[0, i], device(o, xh, y)
            )
            for i, o in enumerate(others_z)
        ]
        for copy in over_z:
            copy.wait_recv()
        total = block[1, here].astype(F32)
        for i in range(reps_z - 1):
            total = total + down_from_z[i].astype(F32)
        down_z[...] = total
        down_y_copies = [
            send(down_z.at[:, o], down_from_y.at[i], b_sem.at[1, i], device(z, xh, o))
            for i, o in enumerate(others_y)
        ]
        return up_z_copies, down_y_copies

    def sum_twice(copies):
        for copy in copies[0] + copies[1]:
            copy.wait_recv()
        total = up_y[here]
        for i in range(reps_z - 1):
            total = total + up_from_z[i]
        pair[:, 0] = total
        total = down_z[:, y]
        for i in range(reps_y - 1):
            total = total + down_from_y[i]
        pair[:, 1] = total
        return send(pair.at[1 - xh], from_x, c_sem.at[0], across)

    def outer_step(copy):
        copy.wait_recv()
        for w, (anchor, moment, cent_out, vel_out) in enumerate(
            (
                (anchor_up, moment_up, central_up, velocity_up),
                (anchor_down, moment_down, central_down, velocity_down),
            )
        ):
            total = pair[xh, w] + from_x[w]
            drift = anchor[...] - total / reps
            velocity = outer_momentum * moment[...] + drift
            cent = anchor[...] - outer_rate * (drift + outer_momentum * velocity)
            vel_out[...] = velocity
            cent_out[...] = cent
            central[w, z * 2 + xh, y] = cent
        mine = central.at[:, z * 2 + xh, y]
        return send(mine, mine, c_sem.at[1], across)

    def gather_once(copy):
        copy.wait_recv()
        up_here = central.at[0, here, y]
        down_here = central.at[1, here, y]
        over_z = [
            send(up_here, up_here, e_sem.at[0, i], device(o, xh, y))
            for i, o in enumerate(others_z)
        ]
        over_y = [
            send(down_here, down_here, e_sem.at[1, i], device(z, xh, o))
            for i, o in enumerate(others_y)
        ]
        return over_z, over_y

    def gather_twice(copies):
        over_z, over_y = copies
        for copy in over_y:
            copy.wait_recv()
        down_here = central.at[1, here]
        out = [
            send(down_here, down_here, f_sem.at[1, i], device(o, xh, y))
            for i, o in enumerate(others_z)
        ]
        for copy in over_z:
            copy.wait_recv()
        up_here = central.at[0, :, y]
        out += [
            send(up_here, up_here, f_sem.at[0, i], device(z, xh, o))
            for i, o in enumerate(others_y)
        ]
        return out

    block_copies = spread_blocks()

    def hidden_of(buf, lo, count, keep_slope):
        rows = slice(lo, lo + count)
        for n, size in pieces(units_here, 256):
            pre = mm(buf[rows, :], up[:, n : n + size]) * (1.0 / math.sqrt(width))
            sig = jax.nn.sigmoid(pre)
            hid[rows, n : n + size] = (pre * sig).astype(BF16)
            if keep_slope:
                slope[rows, n : n + size] = (
                    sig * (1 + pre * (1 - sig)) * (1.0 / math.sqrt(width))
                )

    feats = width // CHUNKS

    def branch_of(lo, count, j):
        part[lo : lo + count, j * feats : (j + 1) * feats] = mm_nt(
            hid[lo : lo + count, :], down[j * feats : (j + 1) * feats, :]
        )

    def sib_send(b, which, j, dst):
        lo = tok + which * half
        cols = pl.ds(j * feats, feats)
        return send(
            part.at[pl.ds(lo, tok), cols],
            dst.at[which, :, cols],
            part_sem.at[b, which, j],
            sib,
        )

    def peer_send(b, j, copy, src_sib, staged, dst):
        copy.wait_recv()
        cols = slice(j * feats, (j + 1) * feats)
        staged[:, cols] = (part[half : half + tok, cols] + src_sib[1, :, cols]).astype(BF16)
        ds = pl.ds(j * feats, feats)
        return send(staged.at[:, ds], dst.at[:, ds], part_sem.at[b, 2, j], peer)

    def lanes_of(column_vector):
        wide = jnp.broadcast_to(column_vector, (tok, 128))
        return jnp.transpose(wide)[0:1, :]

    for near, _ in pairs0:
        near.wait_recv()
    hidden_of(x0, 0, half, True)
    diag0 = []
    near_part0 = []
    for j in range(CHUNKS):
        branch_of(0, half, j)
        near_part0.append(sib_send(0, 0, j, from_sib0))
        diag0.append(forward(x0, 0, j, pairs0[j][1]))
    for copy in diag0:
        copy.wait_recv()
    hidden_of(x0, half, half, True)
    far_part0 = []
    over_part0 = []
    for j in range(CHUNKS):
        branch_of(half, half, j)
        far_part0.append(sib_send(0, 1, j, from_sib0))
        if j:
            over_part0.append(
                peer_send(0, j - 1, far_part0[j - 1], from_sib0, to_peer0, from_peer0)
            )
    over_part0.append(
        peer_send(0, CHUNKS - 1, far_part0[-1], from_sib0, to_peer0, from_peer0)
    )
    for c in range(CHUNKS):
        normalize_chunk(1, x1, c)
    b_copies = sum_once(block_copies)
    for copy in near_part0 + over_part0:
        copy.wait_recv()

    def output_of(b, c, src_sib, src_peer):
        rows = slice(c * rows_each, (c + 1) * rows_each)
        branch = part[rows, :] + src_sib[0, rows, :] + src_peer[rows, :].astype(F32)
        output = x_in[b, rows, :].astype(F32) + branch * (1.0 / math.sqrt(units))
        q = lax.rsqrt(jnp.mean(output * output, axis=-1, keepdims=True) + norm_epsilon)
        c_gain = cot[b, rows, :].astype(F32) * out_gain[...]
        dotted = jnp.sum(c_gain * output, axis=-1, keepdims=True)
        return output, q, c_gain, dotted

    def token_losses(columns):
        return lanes_of(jnp.concatenate(columns, axis=0))

    pairs_d = []
    losses = []
    for c in range(CHUNKS):
        output, q, c_gain, dotted = output_of(0, c, from_sib0, from_peer0)
        losses.append(dotted * q)
        g = c_gain * (1.0 / tokens)
        doutput = q * g - output * (q * q * q * (dotted * (1.0 / (tokens * width))))
        db[c * rows_each : (c + 1) * rows_each, :] = (
            doutput * (1.0 / math.sqrt(units))
        ).astype(BF16)
        pairs_d.append(spread(db, 1, c))
    loss[0:1, :] = token_losses(losses)
    c_copy = sum_twice(b_copies)

    def dpre_of(lo, count):
        rows = slice(lo, lo + count)
        for n, size in pieces(units_here, 256):
            dh = mm(db[rows, :], down[:, n : n + size])
            dpre[rows, n : n + size] = (dh * slope[rows, n : n + size]).astype(BF16)

    step = 256
    n_steps = width // step

    def first_half(dst, left, right):
        def body(i, carry):
            k = pl.multiple_of(i * step, step)
            dst[pl.ds(k, step), :] = mm_tn(left[0:half, pl.ds(k, step)], right[0:half, :])
            return carry

        lax.fori_loop(0, n_steps, body, 0)

    def second_half(w, dst, left, right):
        cols_acc[w] = jnp.zeros((1, units_here), F32)

        def body(i, carry):
            k = pl.multiple_of(i * step, step)
            g = dst[pl.ds(k, step), :] + mm_tn(
                left[half : 2 * half, pl.ds(k, step)], right[half : 2 * half, :]
            )
            dst[pl.ds(k, step), :] = g
            sq = g * g
            cols_acc[w] += jnp.sum(sq, axis=0, keepdims=True)
            lanes = sq[:, 0:128]
            for s in range(128, units_here, 128):
                lanes = lanes + sq[:, s : s + 128]
            rows_out[w, :, pl.ds(k, step)] = jnp.sum(
                jnp.transpose(lanes), axis=0, keepdims=True
            )
            return carry

        lax.fori_loop(0, n_steps, body, 0)
        return [
            send(rows_out.at[w], rows_in.at[w, i], rows_sem.at[w, i], target)
            for i, target in enumerate((sib, peer, diag))
        ]

    for near, _ in pairs_d:
        near.wait_recv()
    dpre_of(0, half)
    diag_d = [forward(db, 1, 0, pairs_d[0][1])]
    first_half(grad_up, x0, dpre)
    diag_d.append(forward(db, 1, 1, pairs_d[1][1]))
    first_half(grad_down, db, hid)
    for c in range(2, CHUNKS):
        diag_d.append(forward(db, 1, c, pairs_d[c][1]))
    d_copy = outer_step(c_copy)
    for copy in diag_d:
        copy.wait_recv()
    pairs1 = [spread(x1, 2, c) for c in range(CHUNKS)]
    dpre_of(half, half)
    rows_up_copies = second_half(0, grad_up, x0, dpre)
    e_copies = gather_once(d_copy)
    diag1 = [forward(x1, 2, c, pairs1[c][1]) for c in range(2)]
    rows_down_copies = second_half(1, grad_down, db, hid)
    f_copies = gather_twice(e_copies)

    def factors(w, copies, rows_ref, cols_ref):
        for copy in copies:
            copy.wait_recv()
        total = rows_out[w] + rows_in[w, 0] + rows_in[w, 1] + rows_in[w, 2]
        rows2 = row_decay * rows_ref[...] + ((1 - row_decay) / units) * total
        cols2 = row_decay * cols_ref[...] + ((1 - row_decay) / width) * cols_acc[w]
        mean = jnp.mean(rows2, axis=-1, keepdims=True)
        rows_in[w, 0] = lax.rsqrt(rows2) * inner_rate
        cols_acc[w] = lax.rsqrt(cols2 / mean)

    def update(w, weight, grad, k, size):
        scale = jnp.transpose(
            jnp.broadcast_to(rows_in[w, 0, :, pl.ds(k, size)], (128, size))
        )
        for s in range(0, units_here, 128):
            move = grad[pl.ds(k, size), s : s + 128] * scale * cols_acc[w, :, s : s + 128]
            old = weight[pl.ds(k, size), s : s + 128].astype(F32)
            weight[pl.ds(k, size), s : s + 128] = (
                old * (1 - inner_rate * weight_decay) - move
            ).astype(BF16)

    def update_all(w, weight, grad):
        def body(i, carry):
            update(w, weight, grad, pl.multiple_of(i * step, step), step)
            return carry

        lax.fori_loop(0, n_steps, body, 0)

    factors(0, rows_up_copies, up_rows, up_cols)
    update_all(0, up, grad_up)
    diag1 += [forward(x1, 2, c, pairs1[c][1]) for c in range(2, CHUNKS)]
    for (near, _), far in zip(pairs1, diag1):
        near.wait_recv()
        far.wait_recv()
    hidden_of(x1, 0, 2 * half, False)
    factors(1, rows_down_copies, down_rows, down_cols)
    for copy in near_part0 + far_part0:
        copy.wait_send()
        sent[:] = [other for other in sent if other is not copy]
    near_part1 = []
    far_part1 = []
    over_part1 = []
    for j in range(CHUNKS):
        for k, size in pieces(feats, step):
            update(1, down, grad_down, j * feats + k, size)
        branch_of(0, 2 * half, j)
        far_part1.append(sib_send(1, 1, j, from_sib1))
        near_part1.append(sib_send(1, 0, j, from_sib1))
        if j:
            over_part1.append(
                peer_send(1, j - 1, far_part1[j - 1], from_sib1, to_peer1, from_peer1)
            )
    over_part1.append(
        peer_send(1, CHUNKS - 1, far_part1[-1], from_sib1, to_peer1, from_peer1)
    )

    for copy in f_copies:
        copy.wait_recv()
    for k in range(0, width, slab):
        for w, (weight, merged) in enumerate(((up, merged_up), (down, merged_down))):
            merged[k : k + slab, :] = (
                mixing * fragment_rows(weight, k, slab).astype(F32)
                + (1 - mixing) * central[w, k // slab].reshape(slab, bw)
            ).astype(BF16)

    for copy in near_part1 + over_part1:
        copy.wait_recv()
    losses = []
    for c in range(CHUNKS):
        _, q, _, dotted = output_of(1, c, from_sib1, from_peer1)
        losses.append(dotted * q)
    loss[1:2, :] = token_losses(losses)
    for copy in sent:
        copy.wait_send()


def hand_over(n, *refs):
    for i in range(n):
        refs[n + i][...] = refs[i][...]


def per_device(reps_z, reps_y, inputs, cotangent, mid_gain, out_gain, up_weight, down_weight,
               up_rows, up_cols, down_rows, down_cols, anchor_up, anchor_down,
               momentum_up, momentum_down, fragment):
    _, _, tok, width = inputs.shape
    units_here = up_weight.shape[2]
    span, bw = anchor_up.shape
    reps = reps_z * 2 * reps_y
    tokens = 4 * tok
    vmem = pl.BlockSpec(memory_space=pltpu.VMEM)
    hbm = pl.BlockSpec(memory_space=pl.ANY)
    smem = pl.BlockSpec(memory_space=pltpu.SMEM)
    flops = 7 * 2 * tokens * width * units_here
    results = pl.pallas_call(
        functools.partial(kernel, reps_z, reps_y),
        out_shape=(
            jax.ShapeDtypeStruct((width, bw), BF16),
            jax.ShapeDtypeStruct((width, bw), BF16),
            jax.ShapeDtypeStruct((span, bw), F32),
            jax.ShapeDtypeStruct((span, bw), F32),
            jax.ShapeDtypeStruct((span, bw), F32),
            jax.ShapeDtypeStruct((span, bw), F32),
            jax.ShapeDtypeStruct((2, tok), F32),
        ),
        in_specs=[smem, vmem, vmem, vmem, vmem, hbm, hbm] + [vmem] * 8,
        out_specs=tuple([vmem] * 7),
        scratch_shapes=[
            pltpu.VMEM((width, units_here), BF16),
            pltpu.VMEM((width, units_here), BF16),
            pltpu.VMEM((tokens, width), BF16),
            pltpu.VMEM((tokens, width), BF16),
            pltpu.VMEM((tokens, width), BF16),
            pltpu.VMEM((tokens, units_here), F32),
            pltpu.VMEM((tokens, units_here), BF16),
            pltpu.VMEM((tokens, units_here), BF16),
            pltpu.VMEM((tokens, width), F32),
            pltpu.VMEM((2, tok, width), F32),
            pltpu.VMEM((2, tok, width), F32),
            pltpu.VMEM((tok, width), BF16),
            pltpu.VMEM((tok, width), BF16),
            pltpu.VMEM((tok, width), BF16),
            pltpu.VMEM((tok, width), BF16),
            pltpu.VMEM((width, units_here), F32),
            pltpu.VMEM((width, units_here), F32),
            pltpu.VMEM((2, 2 * reps_z, reps_y, span, bw), BF16),
            pltpu.VMEM((reps_y - 1, 2 * reps_z, span, bw), BF16),
            pltpu.VMEM((2 * reps_z, span, bw), F32),
            pltpu.VMEM((reps_z - 1, 2, span, bw), F32),
            pltpu.VMEM((reps_z - 1, 2, reps_y, span, bw), BF16),
            pltpu.VMEM((2, reps_y, span, bw), F32),
            pltpu.VMEM((reps_y - 1, 2, span, bw), F32),
            pltpu.VMEM((2, 2, span, bw), F32),
            pltpu.VMEM((2, span, bw), F32),
            pltpu.VMEM((2, 2 * reps_z, reps_y, span, bw), F32),
            pltpu.VMEM((2, 1, width), F32),
            pltpu.VMEM((2, 3, 1, width), F32),
            pltpu.VMEM((2, 1, units_here), F32),
            pltpu.SemaphoreType.DMA((2,)),
            pltpu.SemaphoreType.DMA((3, 3, CHUNKS, 2)),
            pltpu.SemaphoreType.DMA((2, 3, CHUNKS, 2)),
            pltpu.SemaphoreType.DMA((2, 3, 2)),
            pltpu.SemaphoreType.DMA((2, max(reps_y, reps_z) - 1, 2)),
            pltpu.SemaphoreType.DMA((2, max(reps_y, reps_z) - 1, 2)),
            pltpu.SemaphoreType.DMA((2, 2)),
            pltpu.SemaphoreType.DMA((2, max(reps_y, reps_z) - 1, 2)),
            pltpu.SemaphoreType.DMA((2, max(reps_y, reps_z) - 1, 2)),
        ],
        compiler_params=pltpu.CompilerParams(
            collective_id=0,
            has_side_effects=True,
            vmem_limit_bytes=62 * 1024 * 1024,
        ),
        cost_estimate=pl.CostEstimate(
            flops=flops, bytes_accessed=10_000_000, transcendentals=0
        ),
        name="window",
    )(
        fragment,
        inputs[0],
        cotangent[0],
        mid_gain[None],
        out_gain[None],
        up_weight[0],
        down_weight[0],
        up_rows,
        up_cols,
        down_rows,
        down_cols,
        anchor_up,
        anchor_down,
        momentum_up,
        momentum_down,
    )
    results = pl.pallas_call(
        functools.partial(hand_over, len(results)),
        out_shape=tuple(jax.ShapeDtypeStruct(r.shape, r.dtype) for r in results),
        in_specs=[vmem] * len(results),
        out_specs=tuple([vmem] * len(results)),
        name="hand_over",
    )(*results)
    merged_up, merged_down, c_up, c_down, v_up, v_down, loss = results
    return merged_up[None], merged_down[None], c_up, c_down, v_up, v_down, loss[None]


def solution(mesh):
    reps = mesh.shape["rep"]
    reps_y = 4 if reps % 16 == 0 else 2
    reps_z = reps // (2 * reps_y)
    placed = (
        P("rep", None, "fsdp", None),
        P("rep", None, "fsdp", None),
        P(),
        P(),
        P("rep", None, "fsdp"),
        P("rep", None, "fsdp"),
        P("rep", None),
        P("rep", "fsdp"),
        P("rep", None),
        P("rep", "fsdp"),
        P("rep", "fsdp"),
        P("rep", "fsdp"),
        P("rep", "fsdp"),
        P("rep", "fsdp"),
        P(),
    )
    return jax.shard_map(
        functools.partial(per_device, reps_z, reps_y),
        mesh=mesh,
        in_specs=placed,
        out_specs=(
            P("rep", None, "fsdp"),
            P("rep", None, "fsdp"),
            P("rep", "fsdp"),
            P("rep", "fsdp"),
            P("rep", "fsdp"),
            P("rep", "fsdp"),
            P("rep", None, "fsdp"),
        ),
        check_vma=False,
    )
```

```python
import functools
import math

import jax
import jax.numpy as jnp
from jax import lax
from jax.experimental import pallas as pl
from jax.experimental.pallas import tpu as pltpu
from jax.sharding import PartitionSpec as P

norm_epsilon = 1e-05
row_decay = 0.95
inner_rate = 0.05
weight_decay = 0.1
outer_rate = 0.7
outer_momentum = 0.9
mixing = 0.5

F32 = jnp.float32
BF16 = jnp.bfloat16
CHUNKS = 4
GROUPS = 2
FEATS = (2, 2)


def mm(a, b):
    return jnp.dot(a, b, preferred_element_type=F32)


def mm_nt(a, b):
    return lax.dot_general(a, b, (((1,), (1,)), ((), ())), preferred_element_type=F32)


def mm_tn(a, b):
    return lax.dot_general(a, b, (((0,), (0,)), ((), ())), preferred_element_type=F32)


def pieces(extent, size):
    return [(s, min(size, extent - s)) for s in range(0, extent, size)]


def kernel(
    reps_z,
    reps_y,
    frag,
    x_hbm,
    cot_hbm,
    mid_gain,
    out_gain,
    up_hbm,
    down_hbm,
    up_rows,
    up_cols,
    down_rows,
    down_cols,
    anchor_up,
    anchor_down,
    moment_up,
    moment_down,
    merged_up,
    merged_down,
    central_up,
    central_down,
    velocity_up,
    velocity_down,
    loss,
    x_in,
    cot,
    up,
    down,
    x0,
    x1,
    db,
    slope,
    hid,
    dpre,
    part,
    from_sib0,
    from_sib1,
    to_peer0,
    to_peer1,
    from_peer0,
    from_peer1,
    grad_up,
    grad_down,
    block,
    up_from_y,
    up_y,
    up_from_z,
    down_from_z,
    down_z,
    down_from_y,
    pair,
    from_x,
    outer_in,
    central,
    rows_out,
    rows_in,
    cols_acc,
    load_sem,
    gather_sem,
    part_sem,
    rows_sem,
    a_sem,
    b_sem,
    c_sem,
    e_sem,
    f_sem,
    o_sem,
):
    width, units_here = up.shape
    tok = x_hbm.shape[1]
    shards = 4
    units = units_here * shards
    tokens = tok * shards
    reps = reps_z * 2 * reps_y
    group = tokens // GROUPS
    share = tok // GROUPS
    per_group = CHUNKS // GROUPS
    bw = block.shape[4]

    rep = lax.axis_index("rep")
    f = lax.axis_index("fsdp")
    z = rep // (2 * reps_y)
    xh = rep // reps_y % 2
    y = rep % reps_y
    chip = f // 2
    core = f % 2
    sib = {"rep": rep, "fsdp": chip * 2 + (1 - core)}
    peer = {"rep": rep, "fsdp": (1 - chip) * 2 + core}
    diag = {"rep": rep, "fsdp": (1 - chip) * 2 + (1 - core)}

    def device(z_, xh_, y_):
        return {"rep": (z_ * 2 + xh_) * reps_y + y_, "fsdp": f}

    across = device(z, 1 - xh, y)
    others_z = [(z + s) % reps_z for s in range(1, reps_z)]
    others_y = [(y + s) % reps_y for s in range(1, reps_y)]

    sent = []

    def send(src, dst, sems, target):
        copy = pltpu.make_async_remote_copy(
            src_ref=src,
            dst_ref=dst,
            send_sem=sems.at[0],
            recv_sem=sems.at[1],
            device_id=target,
            device_id_type=pl.DeviceIdType.MESH,
        )
        copy.start()
        sent.append(copy)
        return copy

    barrier = pltpu.get_barrier_semaphore()
    partners = [sib, peer, diag]
    partners += [device(o, xh, y) for o in others_z]
    partners += [device(z, xh, o) for o in others_y]
    partners += [across]
    for partner in partners:
        pl.semaphore_signal(
            barrier, inc=1, device_id=partner, device_id_type=pl.DeviceIdType.MESH
        )

    loads = [
        pltpu.make_async_copy(src, dst, load_sem.at[i])
        for i, (src, dst) in enumerate(
            (
                (x_hbm.at[0], x_in.at[0]),
                (up_hbm, up),
                (down_hbm, down),
                (x_hbm.at[1], x_in.at[1]),
                (cot_hbm, cot),
            )
        )
    ]
    for load in loads:
        load.start()

    rows_each = tok // CHUNKS

    def at(c, slot):
        return (c // per_group) * group + slot * share + (c % per_group) * rows_each

    def piece(c, slot):
        return pl.ds(at(c, slot), rows_each)

    def normalize_chunk(batch, dst, c):
        v = x_in[batch, c * rows_each : (c + 1) * rows_each, :].astype(F32)
        factor = lax.rsqrt(jnp.mean(v * v, axis=-1, keepdims=True) + norm_epsilon)
        dst[piece(c, 0), :] = (v * factor * mid_gain[...]).astype(BF16)

    def spread(buf, g, c):
        over = send(
            buf.at[piece(c, 0), :], buf.at[piece(c, 2), :], gather_sem.at[g, 1, c], peer
        )
        near = send(
            buf.at[piece(c, 0), :], buf.at[piece(c, 1), :], gather_sem.at[g, 0, c], sib
        )
        return near, over

    def forward(buf, g, c, pairs):
        pairs[c][1].wait_recv()
        return send(
            buf.at[piece(c, 2), :], buf.at[piece(c, 3), :], gather_sem.at[g, 2, c], sib
        )

    def members(gr):
        return range(gr * per_group, (gr + 1) * per_group)

    loads[0].wait()
    for c in range(per_group):
        normalize_chunk(0, x0, c)
    pl.semaphore_wait(barrier, len(partners))
    pairs0 = [spread(x0, 0, c) for c in range(per_group)]
    for c in range(per_group, CHUNKS):
        normalize_chunk(0, x0, c)
        pairs0.append(spread(x0, 0, c))

    chosen = [jnp.where(frag[0] == k, 1.0, 0.0) for k in range(units_here // bw)]

    def fragment_rows(weight, k, strip):
        rows = pl.ds(k, strip)
        picked = None
        for n, one in enumerate(chosen):
            term = weight[rows, n * bw : (n + 1) * bw] * jnp.full(
                (strip, bw), one, F32
            ).astype(BF16)
            picked = term if picked is None else picked + term
        return picked

    for load in loads[1:]:
        load.wait()
    span = width // reps
    slab = reps_y * span
    for k in range(0, width, slab):
        block[0, k // slab] = fragment_rows(up, k, slab).reshape(reps_y, span, bw)
        block[1, k // slab] = fragment_rows(down, k, slab).reshape(reps_y, span, bw)
    here = pl.ds(z * 2, 2)

    def spread_blocks():
        over_y = [
            send(block.at[0, :, o], up_from_y.at[i], a_sem.at[0, i], device(z, xh, o))
            for i, o in enumerate(others_y)
        ]
        over_z = [
            send(
                block.at[1, pl.ds(o * 2, 2)],
                down_from_z.at[i],
                a_sem.at[1, i],
                device(o, xh, y),
            )
            for i, o in enumerate(others_z)
        ]
        return over_y, over_z

    def sum_once(copies):
        over_y, over_z = copies
        for copy in over_y:
            copy.wait_recv()
        total = block[0, :, y].astype(F32)
        for i in range(reps_y - 1):
            total = total + up_from_y[i].astype(F32)
        up_y[...] = total
        up_z_copies = [
            send(
                up_y.at[pl.ds(o * 2, 2)], up_from_z.at[i], b_sem.at[0, i], device(o, xh, y)
            )
            for i, o in enumerate(others_z)
        ]
        for copy in over_z:
            copy.wait_recv()
        total = block[1, here].astype(F32)
        for i in range(reps_z - 1):
            total = total + down_from_z[i].astype(F32)
        down_z[...] = total
        down_y_copies = [
            send(down_z.at[:, o], down_from_y.at[i], b_sem.at[1, i], device(z, xh, o))
            for i, o in enumerate(others_y)
        ]
        return up_z_copies, down_y_copies

    def sum_twice(copies):
        for copy in copies[0] + copies[1]:
            copy.wait_recv()
        total = up_y[here]
        for i in range(reps_z - 1):
            total = total + up_from_z[i]
        pair[:, 0] = total
        total = down_z[:, y]
        for i in range(reps_y - 1):
            total = total + down_from_y[i]
        pair[:, 1] = total
        return send(pair, from_x, c_sem.at[0], across)

    def outer_step(copy):
        for other in outer_copies + [copy]:
            other.wait_recv()
        for w, (anchor, moment, cent_out, vel_out) in enumerate(
            (
                (anchor_up, moment_up, central_up, velocity_up),
                (anchor_down, moment_down, central_down, velocity_down),
            )
        ):
            for own in (True, False):
                row = xh if own else 1 - xh
                start = anchor[...] if own else outer_in[2 * w]
                speed = moment[...] if own else outer_in[2 * w + 1]
                total = pair[row, w] + from_x[row, w]
                drift = start - total / reps
                velocity = outer_momentum * speed + drift
                cent = start - outer_rate * (drift + outer_momentum * velocity)
                central[w, z * 2 + row, y] = cent
                if own:
                    vel_out[...] = velocity
                    cent_out[...] = cent
        up_here = central.at[0, here, y]
        down_here = central.at[1, here, y]
        over_z = [
            send(up_here, up_here, e_sem.at[0, i], device(o, xh, y))
            for i, o in enumerate(others_z)
        ]
        over_y = [
            send(down_here, down_here, e_sem.at[1, i], device(z, xh, o))
            for i, o in enumerate(others_y)
        ]
        return over_z, over_y

    def gather_twice(copies):
        over_z, over_y = copies
        for copy in over_y:
            copy.wait_recv()
        down_here = central.at[1, here]
        out = [
            send(down_here, down_here, f_sem.at[1, i], device(o, xh, y))
            for i, o in enumerate(others_z)
        ]
        for copy in over_z:
            copy.wait_recv()
        up_here = central.at[0, :, y]
        out += [
            send(up_here, up_here, f_sem.at[0, i], device(z, xh, o))
            for i, o in enumerate(others_y)
        ]
        return out

    block_copies = spread_blocks()
    outer_copies = [
        send(src, outer_in.at[i], o_sem.at[i], across)
        for i, src in enumerate((anchor_up, moment_up, anchor_down, moment_down))
    ]

    def hidden_of(buf, lo, count, keep_slope):
        rows = slice(lo, lo + count)
        for n, size in pieces(units_here, 256):
            pre = mm(buf[rows, :], up[:, n : n + size]) * (1.0 / math.sqrt(width))
            sig = jax.nn.sigmoid(pre)
            hid[rows, n : n + size] = (pre * sig).astype(BF16)
            if keep_slope:
                slope[rows, n : n + size] = (
                    sig * (1 + pre * (1 - sig)) * (1.0 / math.sqrt(width))
                )

    def branch_of(lo, count, j, pieces_n):
        feats = width // pieces_n
        part[lo : lo + count, j * feats : (j + 1) * feats] = mm_nt(
            hid[lo : lo + count, :], down[j * feats : (j + 1) * feats, :]
        )

    def sib_send(b, which, gr, j, dst):
        feats = width // FEATS[b]
        cols = pl.ds(j * feats, feats)
        return send(
            part.at[pl.ds(gr * group + (1 + 2 * which) * share, share), cols],
            dst.at[which, pl.ds(gr * share, share), cols],
            part_sem.at[b, which, gr * FEATS[b] + j],
            sib,
        )

    def peer_send(b, gr, j, copy, src_sib, staged, dst):
        copy.wait_recv()
        feats = width // FEATS[b]
        cols = slice(j * feats, (j + 1) * feats)
        lo = gr * group + 2 * share
        rows = slice(gr * share, (gr + 1) * share)
        staged[rows, cols] = (
            part[lo : lo + share, cols] + src_sib[1, rows, cols]
        ).astype(BF16)
        there = (pl.ds(gr * share, share), pl.ds(j * feats, feats))
        return send(
            staged.at[there], dst.at[there], part_sem.at[b, 2, gr * FEATS[b] + j], peer
        )

    def lanes_of(column_vector):
        wide = jnp.broadcast_to(column_vector, (tok, 128))
        return jnp.transpose(wide)[0:1, :]

    def output_of(b, c, src_sib, src_peer):
        rows = slice(c * rows_each, (c + 1) * rows_each)
        branch = part[piece(c, 0), :] + src_sib[0, rows, :] + src_peer[rows, :].astype(F32)
        output = x_in[b, rows, :].astype(F32) + branch * (1.0 / math.sqrt(units))
        q = lax.rsqrt(jnp.mean(output * output, axis=-1, keepdims=True) + norm_epsilon)
        c_gain = cot[b, rows, :].astype(F32) * out_gain[...]
        dotted = jnp.sum(c_gain * output, axis=-1, keepdims=True)
        return output, q, c_gain, dotted

    def token_losses(columns):
        return lanes_of(jnp.concatenate(columns, axis=0))

    near0 = [[] for _ in range(GROUPS)]
    far0 = [[] for _ in range(GROUPS)]
    over0 = [[] for _ in range(GROUPS)]
    pairs_d = []
    losses = []
    diag0 = [forward(x0, 0, c, pairs0) for c in members(0)]

    def layer_group(gr):
        for c in members(gr):
            pairs0[c][0].wait_recv()
            diag0[c].wait_recv()
        hidden_of(x0, gr * group, group, True)
        n = FEATS[0]
        for j in range(n):
            branch_of(gr * group, group, j, n)
            far0[gr].append(sib_send(0, 1, gr, j, from_sib0))
            near0[gr].append(sib_send(0, 0, gr, j, from_sib0))
            if j:
                over0[gr].append(
                    peer_send(
                        0, gr, j - 1, far0[gr][j - 1], from_sib0, to_peer0, from_peer0
                    )
                )
        if gr + 1 < GROUPS:
            for c in members(gr + 1):
                diag0.append(forward(x0, 0, c, pairs0))
        over0[gr].append(
            peer_send(0, gr, n - 1, far0[gr][n - 1], from_sib0, to_peer0, from_peer0)
        )

    def backward_group(gr):
        for copy in near0[gr] + over0[gr]:
            copy.wait_recv()
        for c in members(gr):
            output, q, c_gain, dotted = output_of(0, c, from_sib0, from_peer0)
            losses.append(dotted * q)
            g = c_gain * (1.0 / tokens)
            doutput = q * g - output * (q * q * q * (dotted * (1.0 / (tokens * width))))
            db[piece(c, 0), :] = (doutput * (1.0 / math.sqrt(units))).astype(BF16)
            pairs_d.append(spread(db, 1, c))

    layer_group(0)
    for c in range(CHUNKS):
        normalize_chunk(1, x1, c)
    layer_group(1)
    b_copies = sum_once(block_copies)
    backward_group(0)
    pairs1 = [spread(x1, 2, 0)]
    backward_group(1)
    c_copy = sum_twice(b_copies)
    loss[0:1, :] = token_losses(losses)

    def dpre_of(lo, count):
        rows = slice(lo, lo + count)
        for n, size in pieces(units_here, 256):
            dh = mm(db[rows, :], down[:, n : n + size])
            dpre[rows, n : n + size] = (dh * slope[rows, n : n + size]).astype(BF16)

    step = min(1024, width)
    n_steps = width // step

    def gradient(gr, dst, left, right):
        lo = gr * group

        def body(i, carry):
            k = pl.multiple_of(i * step, step)
            g = mm_tn(left[lo : lo + group, pl.ds(k, step)], right[lo : lo + group, :])
            if gr:
                g = g + dst[pl.ds(k, step), :]
            dst[pl.ds(k, step), :] = g
            return carry

        lax.fori_loop(0, n_steps, body, 0)

    def last_gradient(w, dst, left, right):
        lo = (GROUPS - 1) * group
        cols_acc[w] = jnp.zeros((1, units_here), F32)

        def body(i, carry):
            k = pl.multiple_of(i * step, step)
            g = dst[pl.ds(k, step), :] + mm_tn(
                left[lo : lo + group, pl.ds(k, step)], right[lo : lo + group, :]
            )
            dst[pl.ds(k, step), :] = g
            sq = g * g
            cols_acc[w] += jnp.sum(sq, axis=0, keepdims=True)
            lanes = sq[:, 0:128]
            for s in range(128, units_here, 128):
                lanes = lanes + sq[:, s : s + 128]
            rows_out[w, :, pl.ds(k, step)] = jnp.sum(
                jnp.transpose(lanes), axis=0, keepdims=True
            )
            return carry

        lax.fori_loop(0, n_steps, body, 0)
        return [
            send(rows_out.at[w], rows_in.at[w, i], rows_sem.at[w, i], target)
            for i, target in enumerate((sib, peer, diag))
        ]

    diag_d = [forward(db, 1, c, pairs_d) for c in members(0)]
    for c in members(0):
        pairs_d[c][0].wait_recv()
        diag_d[c].wait_recv()
    dpre_of(0, group)
    e_copies = outer_step(c_copy)
    gradient(0, grad_up, x0, dpre)
    diag_d.append(forward(db, 1, per_group, pairs_d))
    pairs1.append(spread(x1, 2, 1))
    gradient(0, grad_down, db, hid)
    diag_d += [forward(db, 1, c, pairs_d) for c in members(1)[1:]]
    pairs1 += [spread(x1, 2, c) for c in range(2, CHUNKS)]
    for c in members(1):
        pairs_d[c][0].wait_recv()
        diag_d[c].wait_recv()
    dpre_of(group, group)
    rows_up_copies = last_gradient(0, grad_up, x0, dpre)
    f_copies = gather_twice(e_copies)
    diag1 = [forward(x1, 2, 0, pairs1)]
    rows_down_copies = last_gradient(1, grad_down, db, hid)

    def factors(w, copies, rows_ref, cols_ref):
        for copy in copies:
            copy.wait_recv()
        total = rows_out[w] + rows_in[w, 0] + rows_in[w, 1] + rows_in[w, 2]
        rows2 = row_decay * rows_ref[...] + ((1 - row_decay) / units) * total
        cols2 = row_decay * cols_ref[...] + ((1 - row_decay) / width) * cols_acc[w]
        mean = jnp.mean(rows2, axis=-1, keepdims=True)
        rows_in[w, 0] = lax.rsqrt(rows2) * inner_rate
        cols_acc[w] = lax.rsqrt(cols2 / mean)

    def update(w, weight, grad, k, size):
        scale = jnp.transpose(
            jnp.broadcast_to(rows_in[w, 0, :, pl.ds(k, size)], (128, size))
        )
        for s in range(0, units_here, 128):
            move = grad[pl.ds(k, size), s : s + 128] * scale * cols_acc[w, :, s : s + 128]
            old = weight[pl.ds(k, size), s : s + 128].astype(F32)
            weight[pl.ds(k, size), s : s + 128] = (
                old * (1 - inner_rate * weight_decay) - move
            ).astype(BF16)

    def update_rows(w, weight, grad, lo, count):
        strip = min(count, 256)

        def body(i, carry):
            update(w, weight, grad, pl.multiple_of(lo + i * strip, strip), strip)
            return carry

        lax.fori_loop(0, count // strip, body, 0)

    factors(0, rows_up_copies, up_rows, up_cols)
    update_rows(0, up, grad_up, 0, width)
    diag1 += [forward(x1, 2, c, pairs1) for c in members(0)[1:]]
    for gr in range(GROUPS):
        for copy in near0[gr] + far0[gr]:
            copy.wait_send()
            sent[:] = [other for other in sent if other is not copy]

    near1 = []
    over1 = []

    def second_group(gr):
        for c in members(gr):
            pairs1[c][0].wait_recv()
            diag1[c].wait_recv()
        hidden_of(x1, gr * group, group, False)
        n = FEATS[1]
        far = []
        if gr == 0:
            factors(1, rows_down_copies, down_rows, down_cols)
        for j in range(n):
            if gr == 0:
                update_rows(1, down, grad_down, j * (width // n), width // n)
            branch_of(gr * group, group, j, n)
            far.append(sib_send(1, 1, gr, j, from_sib1))
            near1.append(sib_send(1, 0, gr, j, from_sib1))
            if j:
                over1.append(
                    peer_send(1, gr, j - 1, far[j - 1], from_sib1, to_peer1, from_peer1)
                )
        if gr + 1 < GROUPS:
            for c in members(gr + 1):
                diag1.append(forward(x1, 2, c, pairs1))
        over1.append(peer_send(1, gr, n - 1, far[n - 1], from_sib1, to_peer1, from_peer1))

    for gr in range(GROUPS):
        second_group(gr)

    for copy in f_copies:
        copy.wait_recv()
    for k in range(0, width, slab):
        for w, (weight, merged) in enumerate(((up, merged_up), (down, merged_down))):
            merged[k : k + slab, :] = (
                mixing * fragment_rows(weight, k, slab).astype(F32)
                + (1 - mixing) * central[w, k // slab].reshape(slab, bw)
            ).astype(BF16)

    for copy in near1 + over1:
        copy.wait_recv()
    losses = []
    for c in range(CHUNKS):
        _, q, _, dotted = output_of(1, c, from_sib1, from_peer1)
        losses.append(dotted * q)
    loss[1:2, :] = token_losses(losses)
    for copy in sent:
        copy.wait_send()


def hand_over(n, *refs):
    for i in range(n):
        refs[n + i][...] = refs[i][...]


def per_device(reps_z, reps_y, inputs, cotangent, mid_gain, out_gain, up_weight, down_weight,
               up_rows, up_cols, down_rows, down_cols, anchor_up, anchor_down,
               momentum_up, momentum_down, fragment):
    _, _, tok, width = inputs.shape
    units_here = up_weight.shape[2]
    span, bw = anchor_up.shape
    reps = reps_z * 2 * reps_y
    tokens = 4 * tok
    vmem = pl.BlockSpec(memory_space=pltpu.VMEM)
    hbm = pl.BlockSpec(memory_space=pl.ANY)
    smem = pl.BlockSpec(memory_space=pltpu.SMEM)
    flops = 7 * 2 * tokens * width * units_here
    results = pl.pallas_call(
        functools.partial(kernel, reps_z, reps_y),
        out_shape=(
            jax.ShapeDtypeStruct((width, bw), BF16),
            jax.ShapeDtypeStruct((width, bw), BF16),
            jax.ShapeDtypeStruct((span, bw), F32),
            jax.ShapeDtypeStruct((span, bw), F32),
            jax.ShapeDtypeStruct((span, bw), F32),
            jax.ShapeDtypeStruct((span, bw), F32),
            jax.ShapeDtypeStruct((2, tok), F32),
        ),
        in_specs=[smem, hbm, hbm, vmem, vmem, hbm, hbm] + [vmem] * 8,
        out_specs=tuple([vmem] * 7),
        scratch_shapes=[
            pltpu.VMEM((2, tok, width), BF16),
            pltpu.VMEM((2, tok, width), BF16),
            pltpu.VMEM((width, units_here), BF16),
            pltpu.VMEM((width, units_here), BF16),
            pltpu.VMEM((tokens, width), BF16),
            pltpu.VMEM((tokens, width), BF16),
            pltpu.VMEM((tokens, width), BF16),
            pltpu.VMEM((tokens, units_here), F32),
            pltpu.VMEM((tokens, units_here), BF16),
            pltpu.VMEM((tokens, units_here), BF16),
            pltpu.VMEM((tokens, width), F32),
            pltpu.VMEM((2, tok, width), F32),
            pltpu.VMEM((2, tok, width), F32),
            pltpu.VMEM((tok, width), BF16),
            pltpu.VMEM((tok, width), BF16),
            pltpu.VMEM((tok, width), BF16),
            pltpu.VMEM((tok, width), BF16),
            pltpu.VMEM((width, units_here), F32),
            pltpu.VMEM((width, units_here), F32),
            pltpu.VMEM((2, 2 * reps_z, reps_y, span, bw), BF16),
            pltpu.VMEM((reps_y - 1, 2 * reps_z, span, bw), BF16),
            pltpu.VMEM((2 * reps_z, span, bw), F32),
            pltpu.VMEM((reps_z - 1, 2, span, bw), F32),
            pltpu.VMEM((reps_z - 1, 2, reps_y, span, bw), BF16),
            pltpu.VMEM((2, reps_y, span, bw), F32),
            pltpu.VMEM((reps_y - 1, 2, span, bw), F32),
            pltpu.VMEM((2, 2, span, bw), F32),
            pltpu.VMEM((2, 2, span, bw), F32),
            pltpu.VMEM((4, span, bw), F32),
            pltpu.VMEM((2, 2 * reps_z, reps_y, span, bw), F32),
            pltpu.VMEM((2, 1, width), F32),
            pltpu.VMEM((2, 3, 1, width), F32),
            pltpu.VMEM((2, 1, units_here), F32),
            pltpu.SemaphoreType.DMA((5,)),
            pltpu.SemaphoreType.DMA((3, 3, CHUNKS, 2)),
            pltpu.SemaphoreType.DMA((2, 3, GROUPS * max(FEATS), 2)),
            pltpu.SemaphoreType.DMA((2, 3, 2)),
            pltpu.SemaphoreType.DMA((2, max(reps_y, reps_z) - 1, 2)),
            pltpu.SemaphoreType.DMA((2, max(reps_y, reps_z) - 1, 2)),
            pltpu.SemaphoreType.DMA((2, 2)),
            pltpu.SemaphoreType.DMA((2, max(reps_y, reps_z) - 1, 2)),
            pltpu.SemaphoreType.DMA((2, max(reps_y, reps_z) - 1, 2)),
            pltpu.SemaphoreType.DMA((4, 2)),
        ],
        compiler_params=pltpu.CompilerParams(
            collective_id=0,
            has_side_effects=True,
            vmem_limit_bytes=62 * 1024 * 1024,
        ),
        cost_estimate=pl.CostEstimate(
            flops=flops, bytes_accessed=10_000_000, transcendentals=0
        ),
        name="window",
    )(
        fragment,
        inputs[0],
        cotangent[0],
        mid_gain[None],
        out_gain[None],
        up_weight[0],
        down_weight[0],
        up_rows,
        up_cols,
        down_rows,
        down_cols,
        anchor_up,
        anchor_down,
        momentum_up,
        momentum_down,
    )
    results = pl.pallas_call(
        functools.partial(hand_over, len(results)),
        out_shape=tuple(jax.ShapeDtypeStruct(r.shape, r.dtype) for r in results),
        in_specs=[vmem] * len(results),
        out_specs=tuple([vmem] * len(results)),
        name="hand_over",
    )(*results)
    merged_up, merged_down, c_up, c_down, v_up, v_down, loss = results
    return merged_up[None], merged_down[None], c_up, c_down, v_up, v_down, loss[None]


def solution(mesh):
    reps = mesh.shape["rep"]
    reps_y = 4 if reps % 16 == 0 else 2
    reps_z = reps // (2 * reps_y)
    placed = (
        P("rep", None, "fsdp", None),
        P("rep", None, "fsdp", None),
        P(),
        P(),
        P("rep", None, "fsdp"),
        P("rep", None, "fsdp"),
        P("rep", None),
        P("rep", "fsdp"),
        P("rep", None),
        P("rep", "fsdp"),
        P("rep", "fsdp"),
        P("rep", "fsdp"),
        P("rep", "fsdp"),
        P("rep", "fsdp"),
        P(),
    )
    return jax.shard_map(
        functools.partial(per_device, reps_z, reps_y),
        mesh=mesh,
        in_specs=placed,
        out_specs=(
            P("rep", None, "fsdp"),
            P("rep", None, "fsdp"),
            P("rep", "fsdp"),
            P("rep", "fsdp"),
            P("rep", "fsdp"),
            P("rep", "fsdp"),
            P("rep", None, "fsdp"),
        ),
        check_vma=False,
    )
```

```python
import functools
import math

import jax
import jax.numpy as jnp
from jax import lax
from jax.experimental import pallas as pl
from jax.experimental.pallas import tpu as pltpu
from jax.sharding import PartitionSpec as P

norm_epsilon = 1e-05
row_decay = 0.95
inner_rate = 0.05
weight_decay = 0.1
outer_rate = 0.7
outer_momentum = 0.9
mixing = 0.5

F32 = jnp.float32
BF16 = jnp.bfloat16
CHUNKS = 2
GROUPS = 2
FEATS = (2, 2)


def mm(a, b):
    return jnp.dot(a, b, preferred_element_type=F32)


def mm_nt(a, b):
    return lax.dot_general(a, b, (((1,), (1,)), ((), ())), preferred_element_type=F32)


def mm_tn(a, b):
    return lax.dot_general(a, b, (((0,), (0,)), ((), ())), preferred_element_type=F32)


def pieces(extent, size):
    return [(s, min(size, extent - s)) for s in range(0, extent, size)]


def kernel(
    reps_z,
    reps_y,
    frag,
    x_hbm,
    cot_hbm,
    mid_gain,
    out_gain,
    up_hbm,
    down_hbm,
    up_rows,
    up_cols,
    down_rows,
    down_cols,
    anchor_up,
    anchor_down,
    moment_up,
    moment_down,
    merged_up,
    merged_down,
    central_up,
    central_down,
    velocity_up,
    velocity_down,
    loss,
    x_in,
    cot,
    up,
    down,
    x0,
    x1,
    db,
    slope,
    hid,
    dpre,
    part,
    from_sib0,
    from_sib1,
    to_peer0,
    to_peer1,
    from_peer0,
    from_peer1,
    grad_up,
    grad_down,
    block,
    up_from_y,
    up_y,
    up_from_z,
    down_from_z,
    down_z,
    down_from_y,
    pair,
    from_x,
    outer_in,
    central,
    rows_out,
    rows_in,
    cols_acc,
    load_sem,
    gather_sem,
    part_sem,
    rows_sem,
    a_sem,
    b_sem,
    c_sem,
    e_sem,
    f_sem,
    o_sem,
):
    width, units_here = up.shape
    tok = x_hbm.shape[1]
    shards = 4
    units = units_here * shards
    tokens = tok * shards
    reps = reps_z * 2 * reps_y
    group = tokens // GROUPS
    share = tok // GROUPS
    per_group = CHUNKS // GROUPS
    bw = block.shape[4]

    rep = lax.axis_index("rep")
    f = lax.axis_index("fsdp")
    z = rep // (2 * reps_y)
    xh = rep // reps_y % 2
    y = rep % reps_y
    chip = f // 2
    core = f % 2
    sib = {"rep": rep, "fsdp": chip * 2 + (1 - core)}
    peer = {"rep": rep, "fsdp": (1 - chip) * 2 + core}
    diag = {"rep": rep, "fsdp": (1 - chip) * 2 + (1 - core)}

    def device(z_, xh_, y_):
        return {"rep": (z_ * 2 + xh_) * reps_y + y_, "fsdp": f}

    across = device(z, 1 - xh, y)
    others_z = [(z + s) % reps_z for s in range(1, reps_z)]
    others_y = [(y + s) % reps_y for s in range(1, reps_y)]

    sent = []

    def send(src, dst, sems, target):
        copy = pltpu.make_async_remote_copy(
            src_ref=src,
            dst_ref=dst,
            send_sem=sems.at[0],
            recv_sem=sems.at[1],
            device_id=target,
            device_id_type=pl.DeviceIdType.MESH,
        )
        copy.start()
        sent.append(copy)
        return copy

    barrier = pltpu.get_barrier_semaphore()
    partners = [sib, peer, diag]
    partners += [device(o, xh, y) for o in others_z]
    partners += [device(z, xh, o) for o in others_y]
    partners += [across]
    for partner in partners:
        pl.semaphore_signal(
            barrier, inc=1, device_id=partner, device_id_type=pl.DeviceIdType.MESH
        )

    loads = [
        pltpu.make_async_copy(src, dst, load_sem.at[i])
        for i, (src, dst) in enumerate(
            (
                (x_hbm.at[0], x_in.at[0]),
                (up_hbm, up),
                (down_hbm, down),
                (x_hbm.at[1], x_in.at[1]),
                (cot_hbm, cot),
            )
        )
    ]
    for load in loads:
        load.start()

    rows_each = tok // CHUNKS

    def at(c, slot):
        return (c // per_group) * group + slot * share + (c % per_group) * rows_each

    def piece(c, slot):
        return pl.ds(at(c, slot), rows_each)

    def normalize_chunk(batch, dst, c):
        v = x_in[batch, c * rows_each : (c + 1) * rows_each, :].astype(F32)
        factor = lax.rsqrt(jnp.mean(v * v, axis=-1, keepdims=True) + norm_epsilon)
        dst[piece(c, 0), :] = (v * factor * mid_gain[...]).astype(BF16)

    def spread(buf, g, c):
        over = send(
            buf.at[piece(c, 0), :], buf.at[piece(c, 2), :], gather_sem.at[g, 1, c], peer
        )
        near = send(
            buf.at[piece(c, 0), :], buf.at[piece(c, 1), :], gather_sem.at[g, 0, c], sib
        )
        return near, over

    def forward(buf, g, c, pairs):
        pairs[c][1].wait_recv()
        return send(
            buf.at[piece(c, 2), :], buf.at[piece(c, 3), :], gather_sem.at[g, 2, c], sib
        )

    def members(gr):
        return range(gr * per_group, (gr + 1) * per_group)

    loads[0].wait()
    for c in range(per_group):
        normalize_chunk(0, x0, c)
    pl.semaphore_wait(barrier, len(partners))
    pairs0 = [spread(x0, 0, c) for c in range(per_group)]
    for c in range(per_group, CHUNKS):
        normalize_chunk(0, x0, c)
        pairs0.append(spread(x0, 0, c))

    chosen = [jnp.where(frag[0] == k, 1.0, 0.0) for k in range(units_here // bw)]

    def fragment_rows(weight, k, strip):
        rows = pl.ds(k, strip)
        picked = None
        for n, one in enumerate(chosen):
            term = weight[rows, n * bw : (n + 1) * bw] * jnp.full(
                (strip, bw), one, F32
            ).astype(BF16)
            picked = term if picked is None else picked + term
        return picked

    for load in loads[1:]:
        load.wait()
    span = width // reps
    slab = reps_y * span
    for k in range(0, width, slab):
        block[0, k // slab] = fragment_rows(up, k, slab).reshape(reps_y, span, bw)
        block[1, k // slab] = fragment_rows(down, k, slab).reshape(reps_y, span, bw)
    here = pl.ds(z * 2, 2)

    def spread_blocks():
        over_y = [
            send(block.at[0, :, o], up_from_y.at[i], a_sem.at[0, i], device(z, xh, o))
            for i, o in enumerate(others_y)
        ]
        over_z = [
            send(
                block.at[1, pl.ds(o * 2, 2)],
                down_from_z.at[i],
                a_sem.at[1, i],
                device(o, xh, y),
            )
            for i, o in enumerate(others_z)
        ]
        return over_y, over_z

    def sum_once(copies):
        over_y, over_z = copies
        for copy in over_y:
            copy.wait_recv()
        total = block[0, :, y].astype(F32)
        for i in range(reps_y - 1):
            total = total + up_from_y[i].astype(F32)
        up_y[...] = total
        up_z_copies = [
            send(
                up_y.at[pl.ds(o * 2, 2)], up_from_z.at[i], b_sem.at[0, i], device(o, xh, y)
            )
            for i, o in enumerate(others_z)
        ]
        for copy in over_z:
            copy.wait_recv()
        total = block[1, here].astype(F32)
        for i in range(reps_z - 1):
            total = total + down_from_z[i].astype(F32)
        down_z[...] = total
        down_y_copies = [
            send(down_z.at[:, o], down_from_y.at[i], b_sem.at[1, i], device(z, xh, o))
            for i, o in enumerate(others_y)
        ]
        return up_z_copies, down_y_copies

    def sum_twice(copies):
        for copy in copies[0] + copies[1]:
            copy.wait_recv()
        total = up_y[here]
        for i in range(reps_z - 1):
            total = total + up_from_z[i]
        pair[:, 0] = total
        total = down_z[:, y]
        for i in range(reps_y - 1):
            total = total + down_from_y[i]
        pair[:, 1] = total
        return send(pair, from_x, c_sem.at[0], across)

    def outer_step(copy):
        for other in outer_copies + [copy]:
            other.wait_recv()
        for w, (anchor, moment, cent_out, vel_out) in enumerate(
            (
                (anchor_up, moment_up, central_up, velocity_up),
                (anchor_down, moment_down, central_down, velocity_down),
            )
        ):
            for own in (True, False):
                row = xh if own else 1 - xh
                start = anchor[...] if own else outer_in[2 * w]
                speed = moment[...] if own else outer_in[2 * w + 1]
                total = pair[row, w] + from_x[row, w]
                drift = start - total / reps
                velocity = outer_momentum * speed + drift
                cent = start - outer_rate * (drift + outer_momentum * velocity)
                central[w, z * 2 + row, y] = cent
                if own:
                    vel_out[...] = velocity
                    cent_out[...] = cent
        up_here = central.at[0, here, y]
        down_here = central.at[1, here, y]
        over_z = [
            send(up_here, up_here, e_sem.at[0, i], device(o, xh, y))
            for i, o in enumerate(others_z)
        ]
        over_y = [
            send(down_here, down_here, e_sem.at[1, i], device(z, xh, o))
            for i, o in enumerate(others_y)
        ]
        return over_z, over_y

    def gather_twice(copies):
        over_z, over_y = copies
        for copy in over_y:
            copy.wait_recv()
        down_here = central.at[1, here]
        out = [
            send(down_here, down_here, f_sem.at[1, i], device(o, xh, y))
            for i, o in enumerate(others_z)
        ]
        for copy in over_z:
            copy.wait_recv()
        up_here = central.at[0, :, y]
        out += [
            send(up_here, up_here, f_sem.at[0, i], device(z, xh, o))
            for i, o in enumerate(others_y)
        ]
        return out

    block_copies = spread_blocks()
    outer_copies = [
        send(src, outer_in.at[i], o_sem.at[i], across)
        for i, src in enumerate((anchor_up, moment_up, anchor_down, moment_down))
    ]

    def hidden_of(buf, lo, count, keep_slope):
        rows = slice(lo, lo + count)
        for n, size in pieces(units_here, 256):
            pre = mm(buf[rows, :], up[:, n : n + size]) * (1.0 / math.sqrt(width))
            sig = jax.nn.sigmoid(pre)
            hid[rows, n : n + size] = (pre * sig).astype(BF16)
            if keep_slope:
                slope[rows, n : n + size] = (
                    sig * (1 + pre * (1 - sig)) * (1.0 / math.sqrt(width))
                )

    def branch_of(lo, count, j, pieces_n):
        feats = width // pieces_n
        part[lo : lo + count, j * feats : (j + 1) * feats] = mm_nt(
            hid[lo : lo + count, :], down[j * feats : (j + 1) * feats, :]
        )

    def sib_send(b, which, gr, j, dst):
        feats = width // FEATS[b]
        cols = pl.ds(j * feats, feats)
        return send(
            part.at[pl.ds(gr * group + (1 + 2 * which) * share, share), cols],
            dst.at[which, pl.ds(gr * share, share), cols],
            part_sem.at[b, which, gr * FEATS[b] + j],
            sib,
        )

    def peer_send(b, gr, j, copy, src_sib, staged, dst):
        copy.wait_recv()
        feats = width // FEATS[b]
        cols = slice(j * feats, (j + 1) * feats)
        lo = gr * group + 2 * share
        rows = slice(gr * share, (gr + 1) * share)
        staged[rows, cols] = (
            part[lo : lo + share, cols] + src_sib[1, rows, cols]
        ).astype(BF16)
        there = (pl.ds(gr * share, share), pl.ds(j * feats, feats))
        return send(
            staged.at[there], dst.at[there], part_sem.at[b, 2, gr * FEATS[b] + j], peer
        )

    def lanes_of(column_vector):
        wide = jnp.broadcast_to(column_vector, (tok, 128))
        return jnp.transpose(wide)[0:1, :]

    def output_of(b, c, src_sib, src_peer):
        rows = slice(c * rows_each, (c + 1) * rows_each)
        branch = part[piece(c, 0), :] + src_sib[0, rows, :] + src_peer[rows, :].astype(F32)
        output = x_in[b, rows, :].astype(F32) + branch * (1.0 / math.sqrt(units))
        q = lax.rsqrt(jnp.mean(output * output, axis=-1, keepdims=True) + norm_epsilon)
        c_gain = cot[b, rows, :].astype(F32) * out_gain[...]
        dotted = jnp.sum(c_gain * output, axis=-1, keepdims=True)
        return output, q, c_gain, dotted

    def token_losses(columns):
        return lanes_of(jnp.concatenate(columns, axis=0))

    near0 = [[] for _ in range(GROUPS)]
    far0 = [[] for _ in range(GROUPS)]
    over0 = [[] for _ in range(GROUPS)]
    pairs_d = []
    losses = []
    diag0 = [forward(x0, 0, c, pairs0) for c in members(0)]

    def layer_group(gr):
        for c in members(gr):
            pairs0[c][0].wait_recv()
            diag0[c].wait_recv()
        hidden_of(x0, gr * group, group, True)
        n = FEATS[0]
        for j in range(n):
            branch_of(gr * group, group, j, n)
            far0[gr].append(sib_send(0, 1, gr, j, from_sib0))
            near0[gr].append(sib_send(0, 0, gr, j, from_sib0))
            if j:
                over0[gr].append(
                    peer_send(
                        0, gr, j - 1, far0[gr][j - 1], from_sib0, to_peer0, from_peer0
                    )
                )
        over0[gr].append(
            peer_send(0, gr, n - 1, far0[gr][n - 1], from_sib0, to_peer0, from_peer0)
        )
        if gr + 1 < GROUPS:
            for c in members(gr + 1):
                diag0.append(forward(x0, 0, c, pairs0))

    def backward_group(gr):
        for copy in near0[gr] + over0[gr]:
            copy.wait_recv()
        for c in members(gr):
            output, q, c_gain, dotted = output_of(0, c, from_sib0, from_peer0)
            losses.append(dotted * q)
            g = c_gain * (1.0 / tokens)
            doutput = q * g - output * (q * q * q * (dotted * (1.0 / (tokens * width))))
            db[piece(c, 0), :] = (doutput * (1.0 / math.sqrt(units))).astype(BF16)
            pairs_d.append(spread(db, 1, c))

    layer_group(0)
    for c in range(CHUNKS):
        normalize_chunk(1, x1, c)
    layer_group(1)
    b_copies = sum_once(block_copies)
    backward_group(0)
    pairs1 = []
    backward_group(1)
    c_copy = sum_twice(b_copies)
    loss[0:1, :] = token_losses(losses)

    def dpre_of(lo, count):
        rows = slice(lo, lo + count)
        for n, size in pieces(units_here, 256):
            dh = mm(db[rows, :], down[:, n : n + size])
            dpre[rows, n : n + size] = (dh * slope[rows, n : n + size]).astype(BF16)

    step = min(1024, width)
    n_steps = width // step

    def gradient(gr, dst, left, right):
        lo = gr * group

        def body(i, carry):
            k = pl.multiple_of(i * step, step)
            g = mm_tn(left[lo : lo + group, pl.ds(k, step)], right[lo : lo + group, :])
            if gr:
                g = g + dst[pl.ds(k, step), :]
            dst[pl.ds(k, step), :] = g
            return carry

        lax.fori_loop(0, n_steps, body, 0)

    def last_gradient(w, dst, left, right):
        lo = (GROUPS - 1) * group
        cols_acc[w] = jnp.zeros((1, units_here), F32)

        def body(i, carry):
            k = pl.multiple_of(i * step, step)
            g = dst[pl.ds(k, step), :] + mm_tn(
                left[lo : lo + group, pl.ds(k, step)], right[lo : lo + group, :]
            )
            dst[pl.ds(k, step), :] = g
            sq = g * g
            cols_acc[w] += jnp.sum(sq, axis=0, keepdims=True)
            lanes = sq[:, 0:128]
            for s in range(128, units_here, 128):
                lanes = lanes + sq[:, s : s + 128]
            rows_out[w, :, pl.ds(k, step)] = jnp.sum(
                jnp.transpose(lanes), axis=0, keepdims=True
            )
            return carry

        lax.fori_loop(0, n_steps, body, 0)
        return [
            send(rows_out.at[w], rows_in.at[w, i], rows_sem.at[w, i], target)
            for i, target in enumerate((sib, peer, diag))
        ]

    diag_d = [forward(db, 1, c, pairs_d) for c in members(0)]
    for c in members(0):
        pairs_d[c][0].wait_recv()
        diag_d[c].wait_recv()
    dpre_of(0, group)
    e_copies = outer_step(c_copy)
    gradient(0, grad_up, x0, dpre)
    diag_d.append(forward(db, 1, per_group, pairs_d))
    pairs1 += [spread(x1, 2, c) for c in range(2)]
    gradient(0, grad_down, db, hid)
    diag_d += [forward(db, 1, c, pairs_d) for c in members(1)[1:]]
    pairs1 += [spread(x1, 2, c) for c in range(2, CHUNKS)]
    for c in members(1):
        pairs_d[c][0].wait_recv()
        diag_d[c].wait_recv()
    dpre_of(group, group)
    rows_up_copies = last_gradient(0, grad_up, x0, dpre)
    f_copies = gather_twice(e_copies)
    diag1 = [forward(x1, 2, 0, pairs1)]
    rows_down_copies = last_gradient(1, grad_down, db, hid)

    def factors(w, copies, rows_ref, cols_ref):
        for copy in copies:
            copy.wait_recv()
        total = rows_out[w] + rows_in[w, 0] + rows_in[w, 1] + rows_in[w, 2]
        rows2 = row_decay * rows_ref[...] + ((1 - row_decay) / units) * total
        cols2 = row_decay * cols_ref[...] + ((1 - row_decay) / width) * cols_acc[w]
        mean = jnp.mean(rows2, axis=-1, keepdims=True)
        rows_in[w, 0] = lax.rsqrt(rows2) * inner_rate
        cols_acc[w] = lax.rsqrt(cols2 / mean)

    def update(w, weight, grad, k, size):
        scale = jnp.transpose(
            jnp.broadcast_to(rows_in[w, 0, :, pl.ds(k, size)], (128, size))
        )
        for s in range(0, units_here, 128):
            move = grad[pl.ds(k, size), s : s + 128] * scale * cols_acc[w, :, s : s + 128]
            old = weight[pl.ds(k, size), s : s + 128].astype(F32)
            weight[pl.ds(k, size), s : s + 128] = (
                old * (1 - inner_rate * weight_decay) - move
            ).astype(BF16)

    def update_rows(w, weight, grad, lo, count):
        strip = min(count, 256)

        def body(i, carry):
            update(w, weight, grad, pl.multiple_of(lo + i * strip, strip), strip)
            return carry

        lax.fori_loop(0, count // strip, body, 0)

    factors(0, rows_up_copies, up_rows, up_cols)
    update_rows(0, up, grad_up, 0, width)
    diag1 += [forward(x1, 2, c, pairs1) for c in members(0)[1:]]
    for gr in range(GROUPS):
        for copy in near0[gr] + far0[gr]:
            copy.wait_send()
            sent[:] = [other for other in sent if other is not copy]

    near1 = []
    over1 = []

    def second_group(gr):
        for c in members(gr):
            pairs1[c][0].wait_recv()
            diag1[c].wait_recv()
        hidden_of(x1, gr * group, group, False)
        n = FEATS[1]
        far = []
        if gr == 0:
            factors(1, rows_down_copies, down_rows, down_cols)
        for j in range(n):
            if gr == 0:
                update_rows(1, down, grad_down, j * (width // n), width // n)
            branch_of(gr * group, group, j, n)
            far.append(sib_send(1, 1, gr, j, from_sib1))
            near1.append(sib_send(1, 0, gr, j, from_sib1))
            if j:
                over1.append(
                    peer_send(1, gr, j - 1, far[j - 1], from_sib1, to_peer1, from_peer1)
                )
        over1.append(peer_send(1, gr, n - 1, far[n - 1], from_sib1, to_peer1, from_peer1))
        if gr + 1 < GROUPS:
            for c in members(gr + 1):
                diag1.append(forward(x1, 2, c, pairs1))

    for gr in range(GROUPS):
        second_group(gr)

    for copy in f_copies:
        copy.wait_recv()
    for k in range(0, width, slab):
        for w, (weight, merged) in enumerate(((up, merged_up), (down, merged_down))):
            merged[k : k + slab, :] = (
                mixing * fragment_rows(weight, k, slab).astype(F32)
                + (1 - mixing) * central[w, k // slab].reshape(slab, bw)
            ).astype(BF16)

    for copy in near1 + over1:
        copy.wait_recv()
    losses = []
    for c in range(CHUNKS):
        _, q, _, dotted = output_of(1, c, from_sib1, from_peer1)
        losses.append(dotted * q)
    loss[1:2, :] = token_losses(losses)
    for copy in sent:
        copy.wait_send()


def hand_over(n, *refs):
    for i in range(n):
        refs[n + i][...] = refs[i][...]


def per_device(reps_z, reps_y, inputs, cotangent, mid_gain, out_gain, up_weight, down_weight,
               up_rows, up_cols, down_rows, down_cols, anchor_up, anchor_down,
               momentum_up, momentum_down, fragment):
    _, _, tok, width = inputs.shape
    units_here = up_weight.shape[2]
    span, bw = anchor_up.shape
    reps = reps_z * 2 * reps_y
    tokens = 4 * tok
    vmem = pl.BlockSpec(memory_space=pltpu.VMEM)
    hbm = pl.BlockSpec(memory_space=pl.ANY)
    smem = pl.BlockSpec(memory_space=pltpu.SMEM)
    flops = 7 * 2 * tokens * width * units_here
    results = pl.pallas_call(
        functools.partial(kernel, reps_z, reps_y),
        out_shape=(
            jax.ShapeDtypeStruct((width, bw), BF16),
            jax.ShapeDtypeStruct((width, bw), BF16),
            jax.ShapeDtypeStruct((span, bw), F32),
            jax.ShapeDtypeStruct((span, bw), F32),
            jax.ShapeDtypeStruct((span, bw), F32),
            jax.ShapeDtypeStruct((span, bw), F32),
            jax.ShapeDtypeStruct((2, tok), F32),
        ),
        in_specs=[smem, hbm, hbm, vmem, vmem, hbm, hbm] + [vmem] * 8,
        out_specs=tuple([vmem] * 7),
        scratch_shapes=[
            pltpu.VMEM((2, tok, width), BF16),
            pltpu.VMEM((2, tok, width), BF16),
            pltpu.VMEM((width, units_here), BF16),
            pltpu.VMEM((width, units_here), BF16),
            pltpu.VMEM((tokens, width), BF16),
            pltpu.VMEM((tokens, width), BF16),
            pltpu.VMEM((tokens, width), BF16),
            pltpu.VMEM((tokens, units_here), F32),
            pltpu.VMEM((tokens, units_here), BF16),
            pltpu.VMEM((tokens, units_here), BF16),
            pltpu.VMEM((tokens, width), F32),
            pltpu.VMEM((2, tok, width), F32),
            pltpu.VMEM((2, tok, width), F32),
            pltpu.VMEM((tok, width), BF16),
            pltpu.VMEM((tok, width), BF16),
            pltpu.VMEM((tok, width), BF16),
            pltpu.VMEM((tok, width), BF16),
            pltpu.VMEM((width, units_here), F32),
            pltpu.VMEM((width, units_here), F32),
            pltpu.VMEM((2, 2 * reps_z, reps_y, span, bw), BF16),
            pltpu.VMEM((reps_y - 1, 2 * reps_z, span, bw), BF16),
            pltpu.VMEM((2 * reps_z, span, bw), F32),
            pltpu.VMEM((reps_z - 1, 2, span, bw), F32),
            pltpu.VMEM((reps_z - 1, 2, reps_y, span, bw), BF16),
            pltpu.VMEM((2, reps_y, span, bw), F32),
            pltpu.VMEM((reps_y - 1, 2, span, bw), F32),
            pltpu.VMEM((2, 2, span, bw), F32),
            pltpu.VMEM((2, 2, span, bw), F32),
            pltpu.VMEM((4, span, bw), F32),
            pltpu.VMEM((2, 2 * reps_z, reps_y, span, bw), F32),
            pltpu.VMEM((2, 1, width), F32),
            pltpu.VMEM((2, 3, 1, width), F32),
            pltpu.VMEM((2, 1, units_here), F32),
            pltpu.SemaphoreType.DMA((5,)),
            pltpu.SemaphoreType.DMA((3, 3, CHUNKS, 2)),
            pltpu.SemaphoreType.DMA((2, 3, GROUPS * max(FEATS), 2)),
            pltpu.SemaphoreType.DMA((2, 3, 2)),
            pltpu.SemaphoreType.DMA((2, max(reps_y, reps_z) - 1, 2)),
            pltpu.SemaphoreType.DMA((2, max(reps_y, reps_z) - 1, 2)),
            pltpu.SemaphoreType.DMA((2, 2)),
            pltpu.SemaphoreType.DMA((2, max(reps_y, reps_z) - 1, 2)),
            pltpu.SemaphoreType.DMA((2, max(reps_y, reps_z) - 1, 2)),
            pltpu.SemaphoreType.DMA((4, 2)),
        ],
        compiler_params=pltpu.CompilerParams(
            collective_id=0,
            has_side_effects=True,
            vmem_limit_bytes=62 * 1024 * 1024,
        ),
        cost_estimate=pl.CostEstimate(
            flops=flops, bytes_accessed=10_000_000, transcendentals=0
        ),
        name="window",
    )(
        fragment,
        inputs[0],
        cotangent[0],
        mid_gain[None],
        out_gain[None],
        up_weight[0],
        down_weight[0],
        up_rows,
        up_cols,
        down_rows,
        down_cols,
        anchor_up,
        anchor_down,
        momentum_up,
        momentum_down,
    )
    results = pl.pallas_call(
        functools.partial(hand_over, len(results)),
        out_shape=tuple(jax.ShapeDtypeStruct(r.shape, r.dtype) for r in results),
        in_specs=[vmem] * len(results),
        out_specs=tuple([vmem] * len(results)),
        name="hand_over",
    )(*results)
    merged_up, merged_down, c_up, c_down, v_up, v_down, loss = results
    return merged_up[None], merged_down[None], c_up, c_down, v_up, v_down, loss[None]


def solution(mesh):
    reps = mesh.shape["rep"]
    reps_y = 4 if reps % 16 == 0 else 2
    reps_z = reps // (2 * reps_y)
    placed = (
        P("rep", None, "fsdp", None),
        P("rep", None, "fsdp", None),
        P(),
        P(),
        P("rep", None, "fsdp"),
        P("rep", None, "fsdp"),
        P("rep", None),
        P("rep", "fsdp"),
        P("rep", None),
        P("rep", "fsdp"),
        P("rep", "fsdp"),
        P("rep", "fsdp"),
        P("rep", "fsdp"),
        P("rep", "fsdp"),
        P(),
    )
    return jax.shard_map(
        functools.partial(per_device, reps_z, reps_y),
        mesh=mesh,
        in_specs=placed,
        out_specs=(
            P("rep", None, "fsdp"),
            P("rep", None, "fsdp"),
            P("rep", "fsdp"),
            P("rep", "fsdp"),
            P("rep", "fsdp"),
            P("rep", "fsdp"),
            P("rep", None, "fsdp"),
        ),
        check_vma=False,
    )
```

```python
import functools
import math

import jax
import jax.numpy as jnp
from jax import lax
from jax.experimental import pallas as pl
from jax.experimental.pallas import tpu as pltpu
from jax.sharding import PartitionSpec as P

norm_epsilon = 1e-05
row_decay = 0.95
inner_rate = 0.05
weight_decay = 0.1
outer_rate = 0.7
outer_momentum = 0.9
mixing = 0.5

F32 = jnp.float32
BF16 = jnp.bfloat16
CHUNKS = 2
GROUPS = 2
FEATS = (2, 2)


def mm(a, b):
    return jnp.dot(a, b, preferred_element_type=F32)


def mm_nt(a, b):
    return lax.dot_general(a, b, (((1,), (1,)), ((), ())), preferred_element_type=F32)


def mm_tn(a, b):
    return lax.dot_general(a, b, (((0,), (0,)), ((), ())), preferred_element_type=F32)


def pieces(extent, size):
    return [(s, min(size, extent - s)) for s in range(0, extent, size)]


def kernel(
    reps_z,
    reps_y,
    frag,
    x_hbm,
    cot_hbm,
    mid_gain,
    out_gain,
    up_hbm,
    down_hbm,
    up_rows,
    up_cols,
    down_rows,
    down_cols,
    anchor_up,
    anchor_down,
    moment_up,
    moment_down,
    merged_up,
    merged_down,
    central_up,
    central_down,
    velocity_up,
    velocity_down,
    loss,
    x_in,
    cot,
    up,
    down,
    x0,
    x1,
    db,
    slope,
    hid,
    dpre,
    part,
    from_sib0,
    from_sib1,
    to_peer0,
    to_peer1,
    from_peer0,
    from_peer1,
    grad_up,
    grad_down,
    block,
    up_from_y,
    up_y,
    up_from_z,
    down_from_z,
    down_z,
    down_from_y,
    pair,
    from_x,
    outer_in,
    central,
    rows_out,
    rows_in,
    cols_acc,
    load_sem,
    gather_sem,
    part_sem,
    rows_sem,
    a_sem,
    b_sem,
    c_sem,
    e_sem,
    f_sem,
    o_sem,
):
    width, units_here = up.shape
    tok = x_hbm.shape[1]
    shards = 4
    units = units_here * shards
    tokens = tok * shards
    reps = reps_z * 2 * reps_y
    group = tokens // GROUPS
    share = tok // GROUPS
    per_group = CHUNKS // GROUPS
    bw = block.shape[4]

    rep = lax.axis_index("rep")
    f = lax.axis_index("fsdp")
    z = rep // (2 * reps_y)
    xh = rep // reps_y % 2
    y = rep % reps_y
    chip = f // 2
    core = f % 2
    sib = {"rep": rep, "fsdp": chip * 2 + (1 - core)}
    peer = {"rep": rep, "fsdp": (1 - chip) * 2 + core}
    diag = {"rep": rep, "fsdp": (1 - chip) * 2 + (1 - core)}

    def device(z_, xh_, y_):
        return {"rep": (z_ * 2 + xh_) * reps_y + y_, "fsdp": f}

    across = device(z, 1 - xh, y)
    others_z = [(z + s) % reps_z for s in range(1, reps_z)]
    others_y = [(y + s) % reps_y for s in range(1, reps_y)]

    sent = []

    def send(src, dst, sems, target):
        copy = pltpu.make_async_remote_copy(
            src_ref=src,
            dst_ref=dst,
            send_sem=sems.at[0],
            recv_sem=sems.at[1],
            device_id=target,
            device_id_type=pl.DeviceIdType.MESH,
        )
        copy.start()
        sent.append(copy)
        return copy

    barrier = pltpu.get_barrier_semaphore()
    partners = [sib, peer, diag]
    partners += [device(o, xh, y) for o in others_z]
    partners += [device(z, xh, o) for o in others_y]
    partners += [across]
    for partner in partners:
        pl.semaphore_signal(
            barrier, inc=1, device_id=partner, device_id_type=pl.DeviceIdType.MESH
        )

    loads = [
        pltpu.make_async_copy(src, dst, load_sem.at[i])
        for i, (src, dst) in enumerate(
            (
                (x_hbm.at[0], x_in.at[0]),
                (up_hbm, up),
                (down_hbm, down),
                (x_hbm.at[1], x_in.at[1]),
                (cot_hbm, cot),
            )
        )
    ]
    for load in loads:
        load.start()

    rows_each = tok // CHUNKS

    def at(c, slot):
        return (c // per_group) * group + slot * share + (c % per_group) * rows_each

    def piece(c, slot):
        return pl.ds(at(c, slot), rows_each)

    def normalize_chunk(batch, dst, c):
        v = x_in[batch, c * rows_each : (c + 1) * rows_each, :].astype(F32)
        factor = lax.rsqrt(jnp.mean(v * v, axis=-1, keepdims=True) + norm_epsilon)
        dst[piece(c, 0), :] = (v * factor * mid_gain[...]).astype(BF16)

    def spread(buf, g, c):
        over = send(
            buf.at[piece(c, 0), :], buf.at[piece(c, 2), :], gather_sem.at[g, 1, c], peer
        )
        near = send(
            buf.at[piece(c, 0), :], buf.at[piece(c, 1), :], gather_sem.at[g, 0, c], sib
        )
        return near, over

    def forward(buf, g, c, pairs):
        pairs[c][1].wait_recv()
        return send(
            buf.at[piece(c, 2), :], buf.at[piece(c, 3), :], gather_sem.at[g, 2, c], sib
        )

    def members(gr):
        return range(gr * per_group, (gr + 1) * per_group)

    loads[0].wait()
    for c in range(per_group):
        normalize_chunk(0, x0, c)
    pl.semaphore_wait(barrier, len(partners))
    pairs0 = [spread(x0, 0, c) for c in range(per_group)]
    for c in range(per_group, CHUNKS):
        normalize_chunk(0, x0, c)
        pairs0.append(spread(x0, 0, c))

    chosen = [jnp.where(frag[0] == k, 1.0, 0.0) for k in range(units_here // bw)]

    def fragment_rows(weight, k, strip):
        rows = pl.ds(k, strip)
        picked = None
        for n, one in enumerate(chosen):
            term = weight[rows, n * bw : (n + 1) * bw] * jnp.full(
                (strip, bw), one, F32
            ).astype(BF16)
            picked = term if picked is None else picked + term
        return picked

    for load in loads[1:]:
        load.wait()
    span = width // reps
    slab = reps_y * span
    for k in range(0, width, slab):
        block[0, k // slab] = fragment_rows(up, k, slab).reshape(reps_y, span, bw)
        block[1, k // slab] = fragment_rows(down, k, slab).reshape(reps_y, span, bw)
    here = pl.ds(z * 2, 2)

    def spread_blocks():
        over_y = [
            send(block.at[0, :, o], up_from_y.at[i], a_sem.at[0, i], device(z, xh, o))
            for i, o in enumerate(others_y)
        ]
        over_z = [
            send(
                block.at[1, pl.ds(o * 2, 2)],
                down_from_z.at[i],
                a_sem.at[1, i],
                device(o, xh, y),
            )
            for i, o in enumerate(others_z)
        ]
        return over_y, over_z

    def sum_once(copies):
        over_y, over_z = copies
        for copy in over_y:
            copy.wait_recv()
        total = block[0, :, y].astype(F32)
        for i in range(reps_y - 1):
            total = total + up_from_y[i].astype(F32)
        up_y[...] = total
        up_z_copies = [
            send(
                up_y.at[pl.ds(o * 2, 2)], up_from_z.at[i], b_sem.at[0, i], device(o, xh, y)
            )
            for i, o in enumerate(others_z)
        ]
        for copy in over_z:
            copy.wait_recv()
        total = block[1, here].astype(F32)
        for i in range(reps_z - 1):
            total = total + down_from_z[i].astype(F32)
        down_z[...] = total
        down_y_copies = [
            send(down_z.at[:, o], down_from_y.at[i], b_sem.at[1, i], device(z, xh, o))
            for i, o in enumerate(others_y)
        ]
        return up_z_copies, down_y_copies

    def sum_twice(copies):
        for copy in copies[0] + copies[1]:
            copy.wait_recv()
        total = up_y[here]
        for i in range(reps_z - 1):
            total = total + up_from_z[i]
        pair[:, 0] = total
        total = down_z[:, y]
        for i in range(reps_y - 1):
            total = total + down_from_y[i]
        pair[:, 1] = total
        return send(pair, from_x, c_sem.at[0], across)

    def outer_step(copy):
        for other in outer_copies + [copy]:
            other.wait_recv()
        for w, (anchor, moment, cent_out, vel_out) in enumerate(
            (
                (anchor_up, moment_up, central_up, velocity_up),
                (anchor_down, moment_down, central_down, velocity_down),
            )
        ):
            for own in (True, False):
                row = xh if own else 1 - xh
                start = anchor[...] if own else outer_in[2 * w]
                speed = moment[...] if own else outer_in[2 * w + 1]
                total = pair[row, w] + from_x[row, w]
                drift = start - total / reps
                velocity = outer_momentum * speed + drift
                cent = start - outer_rate * (drift + outer_momentum * velocity)
                central[w, z * 2 + row, y] = cent
                if own:
                    vel_out[...] = velocity
                    cent_out[...] = cent
        up_here = central.at[0, here, y]
        down_here = central.at[1, here, y]
        over_z = [
            send(up_here, up_here, e_sem.at[0, i], device(o, xh, y))
            for i, o in enumerate(others_z)
        ]
        over_y = [
            send(down_here, down_here, e_sem.at[1, i], device(z, xh, o))
            for i, o in enumerate(others_y)
        ]
        return over_z, over_y

    def gather_twice(copies):
        over_z, over_y = copies
        for copy in over_y:
            copy.wait_recv()
        down_here = central.at[1, here]
        out = [
            send(down_here, down_here, f_sem.at[1, i], device(o, xh, y))
            for i, o in enumerate(others_z)
        ]
        for copy in over_z:
            copy.wait_recv()
        up_here = central.at[0, :, y]
        out += [
            send(up_here, up_here, f_sem.at[0, i], device(z, xh, o))
            for i, o in enumerate(others_y)
        ]
        return out

    block_copies = spread_blocks()
    outer_copies = [
        send(src, outer_in.at[i], o_sem.at[i], across)
        for i, src in enumerate((anchor_up, moment_up, anchor_down, moment_down))
    ]

    def hidden_of(buf, lo, count, keep_slope):
        rows = slice(lo, lo + count)
        for n, size in pieces(units_here, 256):
            pre = mm(buf[rows, :], up[:, n : n + size]) * (1.0 / math.sqrt(width))
            sig = jax.nn.sigmoid(pre)
            hid[rows, n : n + size] = (pre * sig).astype(BF16)
            if keep_slope:
                slope[rows, n : n + size] = (
                    sig * (1 + pre * (1 - sig)) * (1.0 / math.sqrt(width))
                )

    def branch_of(lo, count, j, pieces_n):
        feats = width // pieces_n
        part[lo : lo + count, j * feats : (j + 1) * feats] = mm_nt(
            hid[lo : lo + count, :], down[j * feats : (j + 1) * feats, :]
        )

    def sib_send(b, which, gr, j, dst):
        feats = width // FEATS[b]
        cols = pl.ds(j * feats, feats)
        return send(
            part.at[pl.ds(gr * group + (1 + 2 * which) * share, share), cols],
            dst.at[which, pl.ds(gr * share, share), cols],
            part_sem.at[b, which, gr * FEATS[b] + j],
            sib,
        )

    def peer_send(b, gr, j, copy, src_sib, staged, dst):
        copy.wait_recv()
        feats = width // FEATS[b]
        cols = slice(j * feats, (j + 1) * feats)
        lo = gr * group + 2 * share
        rows = slice(gr * share, (gr + 1) * share)
        staged[rows, cols] = (
            part[lo : lo + share, cols] + src_sib[1, rows, cols]
        ).astype(BF16)
        there = (pl.ds(gr * share, share), pl.ds(j * feats, feats))
        return send(
            staged.at[there], dst.at[there], part_sem.at[b, 2, gr * FEATS[b] + j], peer
        )

    def lanes_of(column_vector):
        wide = jnp.broadcast_to(column_vector, (tok, 128))
        return jnp.transpose(wide)[0:1, :]

    def output_of(b, c, src_sib, src_peer):
        rows = slice(c * rows_each, (c + 1) * rows_each)
        branch = part[piece(c, 0), :] + src_sib[0, rows, :] + src_peer[rows, :].astype(F32)
        output = x_in[b, rows, :].astype(F32) + branch * (1.0 / math.sqrt(units))
        q = lax.rsqrt(jnp.mean(output * output, axis=-1, keepdims=True) + norm_epsilon)
        c_gain = cot[b, rows, :].astype(F32) * out_gain[...]
        dotted = jnp.sum(c_gain * output, axis=-1, keepdims=True)
        return output, q, c_gain, dotted

    def token_losses(columns):
        return lanes_of(jnp.concatenate(columns, axis=0))

    near0 = [[] for _ in range(GROUPS)]
    far0 = [[] for _ in range(GROUPS)]
    over0 = [[] for _ in range(GROUPS)]
    pairs_d = []
    losses = []
    diag0 = [forward(x0, 0, c, pairs0) for c in members(0)]

    def layer_group(gr):
        for c in members(gr):
            pairs0[c][0].wait_recv()
            diag0[c].wait_recv()
        hidden_of(x0, gr * group, group, True)
        n = FEATS[0]
        for j in range(n):
            branch_of(gr * group, group, j, n)
            far0[gr].append(sib_send(0, 1, gr, j, from_sib0))
            near0[gr].append(sib_send(0, 0, gr, j, from_sib0))
            if j:
                over0[gr].append(
                    peer_send(
                        0, gr, j - 1, far0[gr][j - 1], from_sib0, to_peer0, from_peer0
                    )
                )
        over0[gr].append(
            peer_send(0, gr, n - 1, far0[gr][n - 1], from_sib0, to_peer0, from_peer0)
        )
        if gr + 1 < GROUPS:
            for c in members(gr + 1):
                diag0.append(forward(x0, 0, c, pairs0))

    def backward_group(gr):
        for copy in near0[gr] + over0[gr]:
            copy.wait_recv()
        for c in members(gr):
            output, q, c_gain, dotted = output_of(0, c, from_sib0, from_peer0)
            losses.append(dotted * q)
            g = c_gain * (1.0 / tokens)
            doutput = q * g - output * (q * q * q * (dotted * (1.0 / (tokens * width))))
            db[piece(c, 0), :] = (doutput * (1.0 / math.sqrt(units))).astype(BF16)
            pairs_d.append(spread(db, 1, c))

    layer_group(0)
    for c in range(CHUNKS):
        normalize_chunk(1, x1, c)
    layer_group(1)
    b_copies = sum_once(block_copies)
    backward_group(0)
    pairs1 = []
    backward_group(1)
    c_copy = sum_twice(b_copies)
    loss[0:1, :] = token_losses(losses)

    def dpre_of(lo, count):
        rows = slice(lo, lo + count)
        for n, size in pieces(units_here, 256):
            dh = mm(db[rows, :], down[:, n : n + size])
            dpre[rows, n : n + size] = (dh * slope[rows, n : n + size]).astype(BF16)

    step = min(1024, width)
    n_steps = width // step

    def gradient(gr, dst, left, right):
        lo = gr * group

        def body(i, carry):
            k = pl.multiple_of(i * step, step)
            g = mm_tn(left[lo : lo + group, pl.ds(k, step)], right[lo : lo + group, :])
            if gr:
                g = g + dst[pl.ds(k, step), :]
            dst[pl.ds(k, step), :] = g
            return carry

        lax.fori_loop(0, n_steps, body, 0)

    def last_gradient(w, dst, left, right):
        lo = (GROUPS - 1) * group
        cols_acc[w] = jnp.zeros((1, units_here), F32)

        def body(i, carry):
            k = pl.multiple_of(i * step, step)
            g = dst[pl.ds(k, step), :] + mm_tn(
                left[lo : lo + group, pl.ds(k, step)], right[lo : lo + group, :]
            )
            dst[pl.ds(k, step), :] = g
            sq = g * g
            cols_acc[w] += jnp.sum(sq, axis=0, keepdims=True)
            lanes = sq[:, 0:128]
            for s in range(128, units_here, 128):
                lanes = lanes + sq[:, s : s + 128]
            rows_out[w, :, pl.ds(k, step)] = jnp.sum(
                jnp.transpose(lanes), axis=0, keepdims=True
            )
            return carry

        lax.fori_loop(0, n_steps, body, 0)
        return [
            send(rows_out.at[w], rows_in.at[w, i], rows_sem.at[w, i], target)
            for i, target in enumerate((sib, peer, diag))
        ]

    diag_d = [forward(db, 1, c, pairs_d) for c in members(0)]
    for c in members(0):
        pairs_d[c][0].wait_recv()
        diag_d[c].wait_recv()
    dpre_of(0, group)
    e_copies = outer_step(c_copy)
    gradient(0, grad_up, x0, dpre)
    diag_d.append(forward(db, 1, per_group, pairs_d))
    pairs1 += [spread(x1, 2, c) for c in range(2)]
    gradient(0, grad_down, db, hid)
    diag_d += [forward(db, 1, c, pairs_d) for c in members(1)[1:]]
    pairs1 += [spread(x1, 2, c) for c in range(2, CHUNKS)]
    for c in members(1):
        pairs_d[c][0].wait_recv()
        diag_d[c].wait_recv()
    dpre_of(group, group)
    rows_up_copies = last_gradient(0, grad_up, x0, dpre)
    f_copies = gather_twice(e_copies)
    diag1 = [forward(x1, 2, 0, pairs1)]
    rows_down_copies = last_gradient(1, grad_down, db, hid)

    def factors(w, copies, rows_ref, cols_ref):
        for copy in copies:
            copy.wait_recv()
        total = rows_out[w] + rows_in[w, 0] + rows_in[w, 1] + rows_in[w, 2]
        rows2 = row_decay * rows_ref[...] + ((1 - row_decay) / units) * total
        cols2 = row_decay * cols_ref[...] + ((1 - row_decay) / width) * cols_acc[w]
        mean = jnp.mean(rows2, axis=-1, keepdims=True)
        rows_in[w, 0] = lax.rsqrt(rows2) * inner_rate
        cols_acc[w] = lax.rsqrt(cols2 / mean)

    def update(w, weight, grad, k, size):
        scale = jnp.transpose(
            jnp.broadcast_to(rows_in[w, 0, :, pl.ds(k, size)], (128, size))
        )
        for s in range(0, units_here, 128):
            move = grad[pl.ds(k, size), s : s + 128] * scale * cols_acc[w, :, s : s + 128]
            old = weight[pl.ds(k, size), s : s + 128].astype(F32)
            weight[pl.ds(k, size), s : s + 128] = (
                old * (1 - inner_rate * weight_decay) - move
            ).astype(BF16)

    def update_rows(w, weight, grad, lo, count):
        strip = min(count, 512)

        def body(i, carry):
            update(w, weight, grad, pl.multiple_of(lo + i * strip, strip), strip)
            return carry

        lax.fori_loop(0, count // strip, body, 0)

    factors(0, rows_up_copies, up_rows, up_cols)
    update_rows(0, up, grad_up, 0, width)
    diag1 += [forward(x1, 2, c, pairs1) for c in members(0)[1:]]
    for gr in range(GROUPS):
        for copy in near0[gr] + far0[gr]:
            copy.wait_send()
            sent[:] = [other for other in sent if other is not copy]

    near1 = []
    over1 = []

    def second_group(gr):
        for c in members(gr):
            pairs1[c][0].wait_recv()
            diag1[c].wait_recv()
        hidden_of(x1, gr * group, group, False)
        n = FEATS[1]
        far = []
        if gr == 0:
            factors(1, rows_down_copies, down_rows, down_cols)
        for j in range(n):
            if gr == 0:
                update_rows(1, down, grad_down, j * (width // n), width // n)
            branch_of(gr * group, group, j, n)
            far.append(sib_send(1, 1, gr, j, from_sib1))
            near1.append(sib_send(1, 0, gr, j, from_sib1))
            if j:
                over1.append(
                    peer_send(1, gr, j - 1, far[j - 1], from_sib1, to_peer1, from_peer1)
                )
        over1.append(peer_send(1, gr, n - 1, far[n - 1], from_sib1, to_peer1, from_peer1))
        if gr + 1 < GROUPS:
            for c in members(gr + 1):
                diag1.append(forward(x1, 2, c, pairs1))

    for gr in range(GROUPS):
        second_group(gr)

    for copy in f_copies:
        copy.wait_recv()
    for k in range(0, width, slab):
        for w, (weight, merged) in enumerate(((up, merged_up), (down, merged_down))):
            merged[k : k + slab, :] = (
                mixing * fragment_rows(weight, k, slab).astype(F32)
                + (1 - mixing) * central[w, k // slab].reshape(slab, bw)
            ).astype(BF16)

    for copy in near1 + over1:
        copy.wait_recv()
    losses = []
    for c in range(CHUNKS):
        _, q, _, dotted = output_of(1, c, from_sib1, from_peer1)
        losses.append(dotted * q)
    loss[1:2, :] = token_losses(losses)
    for copy in sent:
        copy.wait_send()


def hand_over(n, *refs):
    for i in range(n):
        refs[n + i][...] = refs[i][...]


def per_device(reps_z, reps_y, inputs, cotangent, mid_gain, out_gain, up_weight, down_weight,
               up_rows, up_cols, down_rows, down_cols, anchor_up, anchor_down,
               momentum_up, momentum_down, fragment):
    _, _, tok, width = inputs.shape
    units_here = up_weight.shape[2]
    span, bw = anchor_up.shape
    reps = reps_z * 2 * reps_y
    tokens = 4 * tok
    vmem = pl.BlockSpec(memory_space=pltpu.VMEM)
    hbm = pl.BlockSpec(memory_space=pl.ANY)
    smem = pl.BlockSpec(memory_space=pltpu.SMEM)
    flops = 7 * 2 * tokens * width * units_here
    results = pl.pallas_call(
        functools.partial(kernel, reps_z, reps_y),
        out_shape=(
            jax.ShapeDtypeStruct((width, bw), BF16),
            jax.ShapeDtypeStruct((width, bw), BF16),
            jax.ShapeDtypeStruct((span, bw), F32),
            jax.ShapeDtypeStruct((span, bw), F32),
            jax.ShapeDtypeStruct((span, bw), F32),
            jax.ShapeDtypeStruct((span, bw), F32),
            jax.ShapeDtypeStruct((2, tok), F32),
        ),
        in_specs=[smem, hbm, hbm, vmem, vmem, hbm, hbm] + [vmem] * 8,
        out_specs=tuple([vmem] * 7),
        scratch_shapes=[
            pltpu.VMEM((2, tok, width), BF16),
            pltpu.VMEM((2, tok, width), BF16),
            pltpu.VMEM((width, units_here), BF16),
            pltpu.VMEM((width, units_here), BF16),
            pltpu.VMEM((tokens, width), BF16),
            pltpu.VMEM((tokens, width), BF16),
            pltpu.VMEM((tokens, width), BF16),
            pltpu.VMEM((tokens, units_here), F32),
            pltpu.VMEM((tokens, units_here), BF16),
            pltpu.VMEM((tokens, units_here), BF16),
            pltpu.VMEM((tokens, width), F32),
            pltpu.VMEM((2, tok, width), F32),
            pltpu.VMEM((2, tok, width), F32),
            pltpu.VMEM((tok, width), BF16),
            pltpu.VMEM((tok, width), BF16),
            pltpu.VMEM((tok, width), BF16),
            pltpu.VMEM((tok, width), BF16),
            pltpu.VMEM((width, units_here), F32),
            pltpu.VMEM((width, units_here), F32),
            pltpu.VMEM((2, 2 * reps_z, reps_y, span, bw), BF16),
            pltpu.VMEM((reps_y - 1, 2 * reps_z, span, bw), BF16),
            pltpu.VMEM((2 * reps_z, span, bw), F32),
            pltpu.VMEM((reps_z - 1, 2, span, bw), F32),
            pltpu.VMEM((reps_z - 1, 2, reps_y, span, bw), BF16),
            pltpu.VMEM((2, reps_y, span, bw), F32),
            pltpu.VMEM((reps_y - 1, 2, span, bw), F32),
            pltpu.VMEM((2, 2, span, bw), F32),
            pltpu.VMEM((2, 2, span, bw), F32),
            pltpu.VMEM((4, span, bw), F32),
            pltpu.VMEM((2, 2 * reps_z, reps_y, span, bw), F32),
            pltpu.VMEM((2, 1, width), F32),
            pltpu.VMEM((2, 3, 1, width), F32),
            pltpu.VMEM((2, 1, units_here), F32),
            pltpu.SemaphoreType.DMA((5,)),
            pltpu.SemaphoreType.DMA((3, 3, CHUNKS, 2)),
            pltpu.SemaphoreType.DMA((2, 3, GROUPS * max(FEATS), 2)),
            pltpu.SemaphoreType.DMA((2, 3, 2)),
            pltpu.SemaphoreType.DMA((2, max(reps_y, reps_z) - 1, 2)),
            pltpu.SemaphoreType.DMA((2, max(reps_y, reps_z) - 1, 2)),
            pltpu.SemaphoreType.DMA((2, 2)),
            pltpu.SemaphoreType.DMA((2, max(reps_y, reps_z) - 1, 2)),
            pltpu.SemaphoreType.DMA((2, max(reps_y, reps_z) - 1, 2)),
            pltpu.SemaphoreType.DMA((4, 2)),
        ],
        compiler_params=pltpu.CompilerParams(
            collective_id=0,
            has_side_effects=True,
            vmem_limit_bytes=62 * 1024 * 1024,
        ),
        cost_estimate=pl.CostEstimate(
            flops=flops, bytes_accessed=10_000_000, transcendentals=0
        ),
        name="window",
    )(
        fragment,
        inputs[0],
        cotangent[0],
        mid_gain[None],
        out_gain[None],
        up_weight[0],
        down_weight[0],
        up_rows,
        up_cols,
        down_rows,
        down_cols,
        anchor_up,
        anchor_down,
        momentum_up,
        momentum_down,
    )
    results = pl.pallas_call(
        functools.partial(hand_over, len(results)),
        out_shape=tuple(jax.ShapeDtypeStruct(r.shape, r.dtype) for r in results),
        in_specs=[vmem] * len(results),
        out_specs=tuple([vmem] * len(results)),
        name="hand_over",
    )(*results)
    merged_up, merged_down, c_up, c_down, v_up, v_down, loss = results
    return merged_up[None], merged_down[None], c_up, c_down, v_up, v_down, loss[None]


def solution(mesh):
    reps = mesh.shape["rep"]
    reps_y = 4 if reps % 16 == 0 else 2
    reps_z = reps // (2 * reps_y)
    placed = (
        P("rep", None, "fsdp", None),
        P("rep", None, "fsdp", None),
        P(),
        P(),
        P("rep", None, "fsdp"),
        P("rep", None, "fsdp"),
        P("rep", None),
        P("rep", "fsdp"),
        P("rep", None),
        P("rep", "fsdp"),
        P("rep", "fsdp"),
        P("rep", "fsdp"),
        P("rep", "fsdp"),
        P("rep", "fsdp"),
        P(),
    )
    return jax.shard_map(
        functools.partial(per_device, reps_z, reps_y),
        mesh=mesh,
        in_specs=placed,
        out_specs=(
            P("rep", None, "fsdp"),
            P("rep", None, "fsdp"),
            P("rep", "fsdp"),
            P("rep", "fsdp"),
            P("rep", "fsdp"),
            P("rep", "fsdp"),
            P("rep", None, "fsdp"),
        ),
        check_vma=False,
    )
```
